256 devices in a mesh: clip: 8 (over y, core), frame: 32 (over z, x).
Axes of the slice: x: 4, y: 4, z: 8, core: 2. Of those that a mesh axis runs over, the one named last changes fastest.
Arguments:
- visible: bfloat16 [16384, 768], P(('clip', 'frame')), parts along dimension 0, may hold values from -6 to 6
- vis_index: int32 [16384], P(('clip', 'frame')), parts along dimension 0, may hold values from 0 to 25087, as said below
- mask_token: bfloat16 [768], replicated, may hold values from -6 to 6
- time_pos: bfloat16 [32, 768], P('frame'), may hold values from -6 to 6
- space_pos: bfloat16 [784, 768], replicated, may hold values from -6 to 6
- temporal_gain: bfloat16 [768], replicated, may hold values from 0.099609375 to 1.8984375
- temporal_qkv: bfloat16 [768, 2304], replicated, may hold values from -16 to 16
- temporal_out: bfloat16 [768, 768], replicated, may hold values from -0.21875 to 0.21875
- spatial_gain: bfloat16 [768], replicated, may hold values from 0.099609375 to 1.8984375
- spatial_qkv: bfloat16 [768, 2304], replicated, may hold values from -16 to 16
- spatial_out: bfloat16 [768, 768], replicated, may hold values from -0.21875 to 0.21875
Outputs:
- decoded: bfloat16 [256, 784, 768], P(('clip', 'frame')), parts along dimension 0
The draws below stay inside these ranges and needn't reach their ends.
There are 8 independent parts, one for each index of `clip`. The reference program is written for one: setup_inputs(seed, part) draws one part's arguments, and reference() takes and returns one part's arrays. A program takes and returns all parts, laid end to end along the dimension named above; an argument that names none is the same for every part. Nothing has to cross between parts.
Inputs may be any that keep to these rules, and one draw needn't show every extreme that they name: `vis_index`: entries are distinct positions t * 784 + p of one clip. Index j of frame owns time slots j * 1 to (j + 1) - 1; the 64 rows of one index of frame name at most 8 positions of any one owner, and in every draw some owner receives exactly 8 from every index.
All inputs are finite; a program needn't handle non-finite values.
Results may differ from the reference program's by a relative error of at most 0.014.
Values may be sent and summed in bfloat16 or wider, within the bound.
A program may use at most 128 MiB of HBM per device.

```python
import math
import jax
import jax.numpy as jnp
from jax import lax

HEADS = 12
HEAD_DIM = 64
D = 768
P_SIZE = 784
F_DEV = 1
FRAMES = 32
V_DEV = 64
VIS = 2048
CAP = 8
N_FRAME = 32


def draw_vis_index(key, part):
    key = jax.random.fold_in(key, 11)
    heavy_key, place_key, shuffle_key = jax.random.split(key, 3)
    per_owner = F_DEV * P_SIZE
    heavy = jax.random.randint(heavy_key, (), 0, N_FRAME)
    slots = jnp.arange(V_DEV, dtype=jnp.int32)
    remain = jnp.maximum(slots - CAP, 0)
    others = (heavy + 1 + remain % (N_FRAME - 1)) % N_FRAME
    owner = jnp.where(slots < CAP, heavy, others)
    within = jnp.where(slots < CAP, slots, remain // (N_FRAME - 1))
    sources = jnp.arange(N_FRAME, dtype=jnp.int32)
    orders = jax.vmap(lambda inner: jax.random.permutation(inner, per_owner))(jax.random.split(place_key, N_FRAME))
    offset = sources[:, None] * CAP + within[None, :]
    local = orders[jnp.broadcast_to(owner[None, :], offset.shape), offset]
    target = owner[None, :] * per_owner + local
    shuffles = jax.vmap(lambda inner: jax.random.permutation(inner, V_DEV))(jax.random.split(shuffle_key, N_FRAME))
    target = jnp.take_along_axis(target, shuffles, axis=1)
    return target.reshape(-1).astype(jnp.int32)


def draw_temporal_qkv(key, part):
    key = jax.random.fold_in(key, 21)
    base_key = jax.random.fold_in(key, 0)
    matrix = jax.random.truncated_normal(base_key, -6.0, 6.0, (D, 3 * D), jnp.float32) / math.sqrt(D)
    return matrix.astype(jnp.bfloat16)


def draw_spatial_qkv(key, part):
    key = jax.random.fold_in(key, 31)
    base_key = jax.random.fold_in(key, 0)
    matrix = jax.random.truncated_normal(base_key, -6.0, 6.0, (D, 3 * D), jnp.float32) / math.sqrt(D)
    return matrix.astype(jnp.bfloat16)


def block_levels(rng, extent, pieces, low, largest):
    level, own = 1.0, jax.random.fold_in(rng, 6)
    for position, blocks in pieces:
        steps = jnp.exp(jax.random.uniform(jax.random.fold_in(own, position), (blocks,), jnp.float32, low / len(pieces), largest / len(pieces)))
        level = level * jnp.repeat(steps, extent[position] // blocks).reshape([-1 if axis == position else 1 for axis in range(len(extent))])
    return level


def bell_draw(stream_key, dims, deviation, bound, cuts=(), kind=jnp.bfloat16):
    values = deviation * jax.random.normal(stream_key, dims, jnp.float32)
    if cuts:
        values = values * block_levels(stream_key, dims, cuts, -0.22, 0.18)
    return jnp.clip(values, -bound, bound).astype(kind)


def setup_inputs(seed: int = 0, part: int = 0) -> dict:
    splits = jax.random.split(jax.random.key(seed), 12)
    part_keys = jax.random.split(jax.random.fold_in(splits[11], part), 12)
    visible = bell_draw(part_keys[0], (VIS, D), 1.0, 6.0, ((0, 32),))
    vis_index = draw_vis_index(jax.random.fold_in(jax.random.fold_in(splits[11], part), 71), part)
    mask_token = bell_draw(splits[2], (D,), 1.0, 6.0)
    time_pos = bell_draw(splits[3], (FRAMES, D), 1.0, 6.0, ((0, 32),))
    space_pos = bell_draw(splits[4], (P_SIZE, D), 1.0, 6.0)
    temporal_gain = jnp.clip(1.0 + 0.18 * jax.random.normal(splits[5], (D,), jnp.float32), 0.099609375, 1.8984375).astype(jnp.bfloat16)
    temporal_qkv = draw_temporal_qkv(jax.random.fold_in(splits[11], 71), part)
    temporal_out = bell_draw(splits[7], (D, D), D ** -0.5, 0.21875)
    spatial_gain = jnp.clip(1.0 + 0.18 * jax.random.normal(splits[8], (D,), jnp.float32), 0.099609375, 1.8984375).astype(jnp.bfloat16)
    spatial_qkv = draw_spatial_qkv(jax.random.fold_in(splits[11], 71), part)
    spatial_out = bell_draw(splits[10], (D, D), D ** -0.5, 0.21875)
    return {"visible": visible, "vis_index": vis_index, "mask_token": mask_token, "time_pos": time_pos, "space_pos": space_pos, "temporal_gain": temporal_gain, "temporal_qkv": temporal_qkv, "temporal_out": temporal_out, "spatial_gain": spatial_gain, "spatial_qkv": spatial_qkv, "spatial_out": spatial_out}


EPS = 1e-06

def layer_norm(values, gain):
    mean = lax.optimization_barrier(jnp.mean(values, axis=-1, keepdims=True))
    centred = values - mean
    spread = lax.optimization_barrier(jnp.mean(centred * centred, axis=-1, keepdims=True))
    return (centred * lax.rsqrt(spread + EPS) * gain.astype(jnp.float32)).astype(jnp.bfloat16)

def reference(visible, vis_index, mask_token, time_pos, space_pos, temporal_gain, temporal_qkv, temporal_out, spatial_gain, spatial_qkv, spatial_out):
    frames = F_DEV * N_FRAME
    scale = 1.0 / HEAD_DIM ** 0.5
    placed = jnp.broadcast_to(mask_token.astype(jnp.float32)[None, :], (frames * P_SIZE, D))
    placed = placed.at[vis_index].set(visible.astype(jnp.float32))
    tokens = placed.reshape(frames, P_SIZE, D) + time_pos.astype(jnp.float32)[:, None, :]
    tokens = tokens + space_pos.astype(jnp.float32)[None, :, :]
    normed = layer_norm(tokens, temporal_gain)
    time_qkv = jnp.dot(normed.reshape(-1, D), temporal_qkv, preferred_element_type=jnp.float32).astype(jnp.bfloat16)
    time_qkv = time_qkv.reshape(frames, P_SIZE, 3, HEADS, HEAD_DIM).astype(jnp.float32)
    query = time_qkv[:, :, 0]
    keys = time_qkv[:, :, 1]
    values = time_qkv[:, :, 2]
    scores = jnp.einsum('tphd,sphd->phts', query, keys) * scale
    time_probs = jax.nn.softmax(scores, axis=-1).astype(jnp.bfloat16)
    time_mix = jnp.einsum('phts,sphd->tphd', time_probs.astype(jnp.float32), values).astype(jnp.bfloat16)
    after_time = tokens + jnp.dot(time_mix.reshape(-1, D), temporal_out, preferred_element_type=jnp.float32).reshape(frames, P_SIZE, D)
    space_normed = layer_norm(after_time, spatial_gain)
    space_qkv = jnp.dot(space_normed.reshape(-1, D), spatial_qkv, preferred_element_type=jnp.float32).astype(jnp.bfloat16)
    space_qkv = space_qkv.reshape(frames, P_SIZE, 3, HEADS, HEAD_DIM)

    def one_frame(block):
        block = block.astype(jnp.float32)
        frame_scores = jnp.einsum('qhd,khd->hqk', block[:, 0], block[:, 1]) * scale
        frame_probs = jax.nn.softmax(frame_scores, axis=-1).astype(jnp.bfloat16)
        mixed = jnp.einsum('hqk,khd->qhd', frame_probs.astype(jnp.float32), block[:, 2])
        return mixed.astype(jnp.bfloat16).reshape(P_SIZE, D)
    space_mix = lax.map(one_frame, space_qkv)
    decoded = after_time + jnp.dot(space_mix.reshape(-1, D), spatial_out, preferred_element_type=jnp.float32).reshape(frames, P_SIZE, D)
    return decoded.astype(jnp.bfloat16)
```

```python
import functools
import math

import jax
import jax.numpy as jnp
from jax import lax
from jax.experimental import pallas as pl
from jax.experimental.pallas import tpu as pltpu
from jax.sharding import PartitionSpec as P

NX, NZ = 4, 8
FRAMES = NX * NZ
D = 768
HEADS = 12
HEAD_DIM = 64
PATCHES = 784
ROWS = 64
HALF = ROWS // 2
VIS = FRAMES * ROWS
EPS = 1e-6
SCALE = math.log2(math.e) / math.sqrt(HEAD_DIM)
NEG = -1e30
F32 = jnp.float32
BF16 = jnp.bfloat16
NT = (((1,), (1,)), ((), ()))
VMEM = pl.BlockSpec(memory_space=pltpu.VMEM)


class Net:
    def __init__(self, sends, receives):
        self.sends, self.receives, self.started = sends, receives, []

    def send(self, slot, source, target, device):
        copy = pltpu.make_async_remote_copy(
            src_ref=source,
            dst_ref=target,
            send_sem=self.sends.at[slot],
            recv_sem=self.receives.at[slot],
            device_id={"frame": device},
        )
        copy.start()
        self.started.append(copy)

    def wait(self, slot, ref):
        pltpu.make_async_remote_copy(
            src_ref=ref,
            dst_ref=ref,
            send_sem=self.sends.at[slot],
            recv_sem=self.receives.at[slot],
            device_id={"frame": 0},
        ).wait_recv()


def plan():
    events = []
    for half, first in (("A", "x"), ("B", "z")):
        for dz in (0, 1, -1, 2, -2, 3, -3, 4):
            for dx in (0, 1, -1, 2):
                if dz == 0 and dx == 0: continue
                by = ("z" if dz else "x") if half == "A" else ("x" if dx else "z")
                steps = dz if by == "z" else dx
                edge = 4 if by == "z" else 2
                hops = abs(dz) + abs(dx)
                if steps == edge:
                    events.append((hops, half, dz, dx, "lo", by, edge))
                    events.append((hops, half, dz, dx, "hi", by, -edge))
                else:
                    events.append((hops, half, dz, dx, "all", by, steps))
    rank = {"A": 0, "B": 1}
    events.sort(key=lambda e: (e[0], e[5] != "z", rank[e[1]]))
    return events

def gather(net, small_own, a_own, b_own, small, A, B, hooks=lambda k, e: None):
    f = lax.axis_index("frame")
    z, x = f // NX, f % NX
    def zz(d): return lax.rem(z + (d + NZ), NZ)
    def xx(d): return lax.rem(x + (d + NX), NX)
    def place(dz, dx): return xx(dx) * NZ + zz(dz)
    def at(dz, dx): return zz(dz) * NX + xx(dx)
    to = {("x", 1): at(0, 1), ("x", -1): at(0, -1), ("z", 1): at(1, 0), ("z", -1): at(-1, 0)}
    bar = pltpu.get_barrier_semaphore()
    peers = [at(d, 0) for d in range(1, NZ)] + [at(0, d) for d in range(1, NX)]
    for n in peers:
        pl.semaphore_signal(bar, inc=1, device_id={"frame": n})
    hooks("pre", None)
    pl.semaphore_wait(bar, len(peers))
    q = HALF // 2
    part = {"lo": pl.ds(0, q), "hi": pl.ds(q, q), "all": pl.ds(0, HALF)}
    buf = {"A": A, "B": B}
    slots = {}
    def slot(*key):
        return slots.setdefault(key, len(slots))
    def ref(half, dz, dx, p): return buf[half].at[at(-dz, -dx), part[p]]
    def push(half, dz, dx, axis, src=None):
        here = dz if axis == "z" else dx
        edge = 4 if axis == "z" else 2
        for sign in ((1, -1) if here == 0 else ((1,) if here > 0 else (-1,))):
            step = here + sign
            if abs(step) > edge: continue
            ndz, ndx = (step, dx) if axis == "z" else (dz, step)
            p = "all"
            if abs(step) == edge: p = "lo" if step > 0 else "hi"
            key = (half, ndz if abs(ndz) < 4 else 4, ndx if abs(ndx) < 2 else 2, axis, step)
            dst = ref(half, dz, dx, p)
            net.send(slot(*key), dst if src is None else src.at[part[p]], dst, to[axis, sign])
    for d in range(1, NZ):
        net.send(slot("small", "z", d), small_own, small.at[place(0, 0)], at(d, 0))
    push("A", 0, 0, "z", a_own)
    push("B", 0, 0, "x", b_own)
    push("B", 0, 0, "z", b_own)
    push("A", 0, 0, "x", a_own)
    small[place(0, 0)] = small_own[...]
    A[at(0, 0)] = a_own[...]
    B[at(0, 0)] = b_own[...]
    hooks("start", None)
    seen = {}
    columns = small.at[pl.ds(x * NZ, NZ)]
    def small_columns():
        for d in range(1, NZ):
            net.wait(slot("small", "z", d), small.at[place(-d, 0)])
        for d in range(1, NX):
            net.send(slot("small", "x", d), columns, columns, at(0, d))
    def small_rest():
        for d in range(1, NX):
            net.wait(slot("small", "x", d), small.at[pl.ds(xx(-d) * NZ, NZ)])
        hooks("small", None)
    before = 0
    for k, (hops, half, dz, dx, p, axis, step) in enumerate(plan()):
        if hops == 2 and before == 1: small_columns()
        if hops == 3 and before == 2: small_rest()
        before = hops
        net.wait(slot(half, dz, dx, axis, step), ref(half, dz, dx, p))
        seen[half, dz, dx] = seen.get((half, dz, dx), 0) + 1
        whole = p == "all" or seen[half, dz, dx] == 2
        if p == "all":
            push(half, dz, dx, axis)
        if whole:
            if half == "A" and axis == "x": push(half, dz, dx, "z")
            if half == "B" and axis == "z": push(half, dz, dx, "x")
        hooks(k, (half, dz, dx, whole))
    hooks("end", None)
    for c in net.started: c.wait_send()

def gather_kernel(small_own, visible, small, A, B, sends, receives):
    gather(
        Net(sends, receives),
        small_own,
        visible.at[pl.ds(0, HALF)],
        visible.at[pl.ds(HALF, HALF)],
        small,
        A,
        B,
    )


def gather_rows(small_own, visible):
    return pl.pallas_call(
        gather_kernel,
        out_shape=[
            jax.ShapeDtypeStruct((FRAMES, 8, 128), F32),
            jax.ShapeDtypeStruct((FRAMES, HALF, D), BF16),
            jax.ShapeDtypeStruct((FRAMES, HALF, D), BF16),
        ],
        in_specs=[VMEM] * 2,
        out_specs=[VMEM] * 3,
        scratch_shapes=[pltpu.SemaphoreType.DMA((96,)), pltpu.SemaphoreType.DMA((96,))],
        compiler_params=pltpu.CompilerParams(
            collective_id=0, has_side_effects=True, vmem_limit_bytes=56 << 20
        ),
        name="gather_rows",
    )(small_own, visible)


def dot(a, b, precision=None):
    return jnp.dot(a, b, preferred_element_type=F32, precision=precision)


def dot_nt(a, b, precision=None):
    return lax.dot_general(a, b, NT, preferred_element_type=F32, precision=precision)


def iota(shape, axis):
    return lax.broadcasted_iota(jnp.int32, shape, axis)


def normalise(values, gain):
    centred = values - jnp.mean(values, axis=-1, keepdims=True)
    spread = jnp.mean(centred * centred, axis=-1, keepdims=True)
    return (centred * lax.rsqrt(spread + EPS) * gain).astype(BF16)


def split(values):
    high = values.astype(BF16)
    return jnp.concatenate([high, (values - high.astype(F32)).astype(BF16)], axis=1)


def over_slots(values, op):
    for shift in (64, 32, 16):
        values = op(values, pltpu.roll(values, shift, 1))
    return values


def temporal_kernel(
    slot_col,
    patch_col,
    slot_row,
    patch_row,
    patch_list,
    rows,
    times,
    mask,
    space,
    gain,
    qkv,
    out_weight,
    after,
    pick,
    put,
    bk,
    bv,
    kv,
    tokens,
    query,
    scores,
    rs,
    sees,
    top,
    rowscore,
    rowtop,
    weighted,
    rowexp,
    mixed,
    row_kv,
):
    me = lax.axis_index("frame")
    g = gain[...].astype(F32)
    m = mask[...].astype(F32)
    HI = lax.Precision.HIGHEST
    step = 256
    real = pl.ds(0, PATCHES)
    for i in range(VIS // step):
        part = pl.ds(i * step, step)
        pick[part, :] = (patch_col[part, :] == iota((step, WIDE), 1)).astype(BF16)
    put[...] = (patch_row[...] == iota((PATCHES, VIS), 0)).astype(BF16)
    b = space[...].astype(F32)
    b = b - jnp.mean(b, axis=-1, keepdims=True)
    bg = (b * g).astype(BF16)
    a = times[...] + m
    a = a - jnp.mean(a, axis=-1, keepdims=True)
    ag = (a * g).astype(BF16)
    for n in range(3):
        cols = pl.ds(n * 256, 256)
        bk[:, cols] = dot(bg, qkv[:, pl.ds(D + n * 256, 256)])
        bv[:, cols] = dot(bg, qkv[:, pl.ds(2 * D + n * 256, 256)])
    own_head = iota((FRAMES * 16, D), 0) % 16 == iota((FRAMES * 16, D), 1) // HEAD_DIM
    for n in range(2):
        part = dot(ag, qkv[:, pl.ds(D + n * D, D)])
        part = jnp.broadcast_to(part[:, None, :], (FRAMES, 16, D)).reshape(FRAMES * 16, D)
        kv[n] = jnp.where(own_head, part, 0.0).astype(BF16)
    aa = dot_nt(jnp.ones((8, D), F32), a * a, HI)[0:1, :]
    bb = jnp.sum(b * b, axis=-1, keepdims=True)
    spread = jnp.maximum(dot_nt(b, a, HI) * 2.0 + (aa + bb), 0.0) * (1.0 / D)
    r = lax.rsqrt(spread + EPS)
    widen = (iota((FRAMES, FRAMES * 16), 0) == iota((FRAMES, FRAMES * 16), 1) // 16).astype(BF16)
    r_hi = r.astype(BF16)
    r_lo = r - r_hi.astype(F32)
    r_mid = r_lo.astype(BF16)
    r_lo = (r_lo - r_mid.astype(F32)).astype(BF16)
    rs[...] = dot(r_hi, widen) + dot(r_mid, widen) + dot(r_lo, widen)
    is_slot = (slot_col[...] == iota((VIS, FRAMES), 1)).astype(BF16)
    seen = dot(put[...], is_slot)
    sees[...] = dot(seen.astype(BF16), widen)
    own_seen = jnp.sum(jnp.where(iota((PATCHES, FRAMES), 1) == me, seen, 0.0), axis=1, keepdims=True)
    times_b = times[...].astype(BF16)
    space_b = jnp.concatenate([space[...], jnp.zeros((WIDE - PATCHES, D), BF16)], axis=0)
    query[pl.ds(PATCHES, WIDE - PATCHES), :] = jnp.zeros((WIDE - PATCHES, D), BF16)
    top[pl.ds(PATCHES, WIDE - PATCHES), :] = jnp.zeros((WIDE - PATCHES, 128), F32)
    for i in range(VIS // step):
        part = pl.ds(i * step, step)
        where_slot = (slot_col[part, :] == iota((step, FRAMES), 1)).astype(BF16)
        tok = rows[part, :].astype(F32) + dot(where_slot, times_b)
        tok = tok + dot(pick[part, :], space_b)
        row_kv[part, :] = normalise(tok, g)
    for n in range(6):
        cols = pl.ds(n * 256, 256)
        target = weighted if n < 3 else rowexp
        target[:, pl.ds((n % 3) * 256, 256)] = dot(row_kv[...], qkv[:, pl.ds(D + n * 256, 256)]).astype(BF16)
    mine = jnp.where(slot_row[...] == me, put[...], jnp.zeros((), BF16))
    placed = dot(mine, rows[...])
    own_time = jnp.sum(jnp.where(iota((FRAMES, D), 0) == me, times[...], 0.0), axis=0, keepdims=True)
    tokens[...] = jnp.where(own_seen > 0.5, placed, m) + own_time + space[...].astype(F32)
    own_normed = normalise(tokens[...], g)
    for n in range(3):
        cols = pl.ds(n * 256, 256)
        query[real, cols] = dot(own_normed, qkv[:, cols]).astype(BF16)
    of_head = (iota((D, 128), 0) // HEAD_DIM == iota((D, 128), 1) % 16).astype(BF16)
    to_head = (iota((128, D), 0) == iota((128, D), 1) // HEAD_DIM).astype(BF16)
    to_head2 = jnp.concatenate([to_head, to_head], axis=0)
    both = dot((query[real, :].astype(F32) * bk[...]).astype(BF16), of_head)
    high = jnp.full((PATCHES, 128), NEG, F32)
    for n in range(4):
        cols = pl.ds(n * 128, 128)
        scale = rs[:, cols] * SCALE
        part = dot_nt(query[real, :], kv[0, cols, :]) * scale + both * scale
        scores[:, cols] = part
        high = jnp.maximum(high, jnp.where(sees[:, cols] > 0.5, NEG, part))
    top[real, :] = over_slots(high, jnp.maximum)
    top_b = top[...].astype(BF16)
    for i in range(VIS // step):
        part = pl.ds(i * step, step)
        got = dot(pick[part, :], query[...])
        rowscore[part, :] = dot((got * weighted[part, :].astype(F32)).astype(BF16), of_head) * SCALE
        rowtop[part, :] = dot(pick[part, :], top_b)
    over = jnp.max(rowscore[...] - rowtop[...])
    under = jnp.min(top[real, :])

    @pl.when((over > 60.0) | (under < -1e29))
    def _():
        @pl.loop(0, VIS)
        def _(i):
            p = patch_list[i]
            top[pl.ds(p, 1), :] = jnp.maximum(top[pl.ds(p, 1), :], rowscore[pl.ds(i, 1), :])

        for i in range(VIS // step):
            part = pl.ds(i * step, step)
            rowtop[part, :] = dot(pick[part, :], top[...].astype(BF16))

    peak = top[real, :].astype(BF16).astype(F32)
    total = jnp.zeros((PATCHES, 128), F32)
    total_r = jnp.zeros((PATCHES, 128), F32)
    for n in range(4):
        cols = pl.ds(n * 128, 128)
        e = jnp.where(sees[:, cols] > 0.5, 0.0, jnp.exp2(scores[:, cols] - peak))
        total = total + e
        e = e * rs[:, cols]
        total_r = total_r + e
        mixed[:, cols] = e.astype(BF16)
    total = over_slots(total, jnp.add)
    total_r = over_slots(total_r, jnp.add)
    for i in range(VIS // step):
        part = pl.ds(i * step, step)
        e = jnp.exp2(rowscore[part, :] - rowtop[part, :]).astype(BF16)
        weighted[part, pl.ds(0, 128)] = e
        row_kv[part, :] = (dot(e, to_head) * rowexp[part, :].astype(F32)).astype(BF16)
    total = total + dot(put[...], weighted[:, pl.ds(0, 128)])
    share = split(1.0 / total)
    spill = split(total_r)
    for n in range(3):
        cols = pl.ds(n * 256, 256)
        value = dot(mixed[:, pl.ds(0, 512)], kv[1, :, cols])
        value = value + dot(spill, to_head2[:, n * 256 : n * 256 + 256]) * bv[:, cols]
        value = value + dot(put[...], row_kv[:, cols])
        value = value * dot(share, to_head2[:, n * 256 : n * 256 + 256])
        query[real, cols] = value.astype(BF16)
    for n in range(3):
        cols = pl.ds(n * 256, 256)
        after[:, cols] = tokens[:, cols] + dot(query[real, :], out_weight[:, cols])


def temporal(slot, patch, rows, times, mask, space, gain, qkv, out_weight):
    smem = pl.BlockSpec(memory_space=pltpu.SMEM)
    return pl.pallas_call(
        temporal_kernel,
        out_shape=jax.ShapeDtypeStruct((PATCHES, D), F32),
        in_specs=[VMEM] * 4 + [smem] + [VMEM] * 7,
        out_specs=VMEM,
        scratch_shapes=[
            pltpu.VMEM((VIS, WIDE), BF16),
            pltpu.VMEM((PATCHES, VIS), BF16),
            pltpu.VMEM((PATCHES, D), F32),
            pltpu.VMEM((PATCHES, D), F32),
            pltpu.VMEM((2, FRAMES * 16, D), BF16),
            pltpu.VMEM((PATCHES, D), F32),
            pltpu.VMEM((WIDE, D), BF16),
            pltpu.VMEM((PATCHES, 512), F32),
            pltpu.VMEM((PATCHES, 512), F32),
            pltpu.VMEM((PATCHES, 512), F32),
            pltpu.VMEM((WIDE, 128), F32),
            pltpu.VMEM((VIS, 128), F32),
            pltpu.VMEM((VIS, 128), F32),
            pltpu.VMEM((VIS, D), BF16),
            pltpu.VMEM((VIS, D), BF16),
            pltpu.VMEM((PATCHES, 512), BF16),
            pltpu.VMEM((VIS, D), BF16),
        ],
        compiler_params=pltpu.CompilerParams(vmem_limit_bytes=60 << 20),
        name="temporal",
    )(
        slot[:, None],
        patch[:, None],
        slot[None, :],
        patch[None, :],
        patch,
        rows,
        times,
        mask[None, :],
        space,
        gain[None, :],
        qkv,
        out_weight,
    )


CHUNK = 112
WIDE = 896
UNROLL = 7


def spatial_kernel(after, gain, qkv, out_weight, decoded, normed, heads, mixed):
    g = gain[...].astype(F32)

    @pl.loop(0, PATCHES // CHUNK)
    def _(i):
        part = pl.ds(pl.multiple_of(i * CHUNK, CHUNK), CHUNK)
        normed[part, :] = normalise(after[part, :], g)

    heads[pl.ds(PATCHES, WIDE - PATCHES), :] = jnp.zeros((WIDE - PATCHES, 3 * D), BF16)

    @pl.loop(0, 9)
    def _(n):
        cols = pl.ds(pl.multiple_of(n * 256, 256), 256)
        scale = jnp.where(n < 3, SCALE, 1.0)
        heads[pl.ds(0, PATCHES), cols] = (dot(normed[...], qkv[:, cols]) * scale).astype(BF16)

    left = (iota((1, 128), 1) < HEAD_DIM).astype(BF16)
    right = (iota((1, 128), 1) >= HEAD_DIM).astype(BF16)
    real = (iota((WIDE, 1), 0) < PATCHES).astype(BF16)
    tail = iota((1, 128), 1) < PATCHES - (WIDE - 128)

    @pl.loop(0, HEADS // 2)
    def _(pair):
        def lanes(base):
            return pl.ds(pl.multiple_of(base + pair * 128, 128), 128)

        keys = heads[:, lanes(D)]
        values = heads[:, lanes(2 * D)]
        sides = [
            (side, jnp.concatenate([values * side, real * side], axis=1))
            for side in (left, right)
        ]

        @pl.loop(0, PATCHES // CHUNK, unroll=UNROLL)
        def _(i):
            part = pl.ds(pl.multiple_of(i * CHUNK, CHUNK), CHUNK)
            found = jnp.zeros((CHUNK, 256), F32)
            for side, value in sides:
                s = dot_nt(heads[part, lanes(0)] * side, keys)
                s = jnp.concatenate(
                    [s[:, : WIDE - 128], jnp.where(tail, s[:, WIDE - 128 :], NEG)], axis=1
                )
                s = jnp.exp2(s - jnp.max(s, axis=1, keepdims=True)).astype(BF16)
                found = found + dot(s, value)
            mixed[part, lanes(0)] = (found[:, :128] / found[:, 128:]).astype(BF16)

    @pl.loop(0, 3)
    def _(n):
        cols = pl.ds(pl.multiple_of(n * 256, 256), 256)
        decoded[:, cols] = (after[:, cols] + dot(mixed[...], out_weight[:, cols])).astype(BF16)


def spatial(after, gain, qkv, out_weight):
    return pl.pallas_call(
        spatial_kernel,
        out_shape=jax.ShapeDtypeStruct((PATCHES, D), BF16),
        in_specs=[VMEM] * 4,
        out_specs=VMEM,
        scratch_shapes=[
            pltpu.VMEM((PATCHES, D), BF16),
            pltpu.VMEM((WIDE, 3 * D), BF16),
            pltpu.VMEM((PATCHES, D), BF16),
        ],
        compiler_params=pltpu.CompilerParams(vmem_limit_bytes=56 << 20),
        name="spatial",
    )(after, gain[None, :], qkv, out_weight)


def body(
    visible,
    vis_index,
    mask_token,
    time_pos,
    space_pos,
    temporal_gain,
    temporal_qkv,
    temporal_out,
    spatial_gain,
    spatial_qkv,
    spatial_out,
):
    where = jnp.pad(vis_index.astype(F32), (0, 128 - ROWS)).reshape(1, 128)
    small_own = jnp.concatenate(
        [time_pos.astype(F32).reshape(D // 128, 128), where, jnp.zeros((1, 128), F32)], axis=0
    )
    small, first, second = gather_rows(small_own, visible)
    small = small.reshape(NX, NZ, 8, 128).transpose(1, 0, 2, 3).reshape(FRAMES, 8, 128)
    times = small[:, : D // 128].reshape(FRAMES, D)
    index = small[:, 6, :ROWS].astype(jnp.int32)
    index = jnp.concatenate([index[:, :HALF].reshape(-1), index[:, HALF:].reshape(-1)])
    rows = jnp.concatenate([first.reshape(-1, D), second.reshape(-1, D)], axis=0)
    slot = index // PATCHES
    patch = index - slot * PATCHES
    after = temporal(
        slot, patch, rows, times, mask_token, space_pos, temporal_gain, temporal_qkv, temporal_out
    )
    return spatial(after, spatial_gain, spatial_qkv, spatial_out)[None]


def solution(mesh):
    in_specs = (
        P(("clip", "frame"), None),
        P(("clip", "frame")),
        P(),
        P("frame", None),
        P(),
        P(),
        P(),
        P(),
        P(),
        P(),
        P(),
    )
    out_specs = P(("clip", "frame"), None, None)
    return jax.shard_map(body, mesh=mesh, in_specs=in_specs, out_specs=out_specs, check_vma=False)
```

```python
import functools
import math

import jax
import jax.numpy as jnp
from jax import lax
from jax.experimental import pallas as pl
from jax.experimental.pallas import tpu as pltpu
from jax.sharding import PartitionSpec as P

NX, NZ = 4, 8
FRAMES = NX * NZ
D = 768
HEADS = 12
HEAD_DIM = 64
PATCHES = 784
ROWS = 64
HALF = ROWS // 2
VIS = FRAMES * ROWS
EPS = 1e-6
SCALE = math.log2(math.e) / math.sqrt(HEAD_DIM)
NEG = -1e30
F32 = jnp.float32
BF16 = jnp.bfloat16
NT = (((1,), (1,)), ((), ()))
VMEM = pl.BlockSpec(memory_space=pltpu.VMEM)
HBM = pl.BlockSpec(memory_space=pl.ANY)


class Net:
    def __init__(self, sends, receives):
        self.sends, self.receives, self.started = sends, receives, []

    def send(self, slot, source, target, device):
        copy = pltpu.make_async_remote_copy(
            src_ref=source,
            dst_ref=target,
            send_sem=self.sends.at[slot],
            recv_sem=self.receives.at[slot],
            device_id={"frame": device},
        )
        copy.start()
        self.started.append(copy)

    def wait(self, slot, ref):
        pltpu.make_async_remote_copy(
            src_ref=ref,
            dst_ref=ref,
            send_sem=self.sends.at[slot],
            recv_sem=self.receives.at[slot],
            device_id={"frame": 0},
        ).wait_recv()


def plan():
    events = []
    for half, first in (("A", "x"), ("B", "z")):
        for dz in (0, 1, -1, 2, -2, 3, -3, 4):
            for dx in (0, 1, -1, 2):
                if dz == 0 and dx == 0: continue
                by = ("z" if dz else "x") if half == "A" else ("x" if dx else "z")
                steps = dz if by == "z" else dx
                edge = 4 if by == "z" else 2
                hops = abs(dz) + abs(dx)
                if steps == edge:
                    events.append((hops, half, dz, dx, "lo", by, edge))
                    events.append((hops, half, dz, dx, "hi", by, -edge))
                else:
                    events.append((hops, half, dz, dx, "all", by, steps))
    rank = {"A": 0, "B": 1}
    events.sort(key=lambda e: (e[0], e[5] != "z", rank[e[1]]))
    return events

def gather(net, small_own, a_own, b_own, small, A, B, hooks=lambda k, e: None):
    f = lax.axis_index("frame")
    z, x = f // NX, f % NX
    def zz(d): return lax.rem(z + (d + NZ), NZ)
    def xx(d): return lax.rem(x + (d + NX), NX)
    def place(dz, dx): return xx(dx) * NZ + zz(dz)
    def at(dz, dx): return zz(dz) * NX + xx(dx)
    to = {("x", 1): at(0, 1), ("x", -1): at(0, -1), ("z", 1): at(1, 0), ("z", -1): at(-1, 0)}
    bar = pltpu.get_barrier_semaphore()
    peers = [at(d, 0) for d in range(1, NZ)] + [at(0, d) for d in range(1, NX)]
    for n in peers:
        pl.semaphore_signal(bar, inc=1, device_id={"frame": n})
    hooks("pre", None)
    pl.semaphore_wait(bar, len(peers))
    q = HALF // 2
    part = {"lo": pl.ds(0, q), "hi": pl.ds(q, q), "all": pl.ds(0, HALF)}
    buf = {"A": A, "B": B}
    slots = {}
    def slot(*key):
        return slots.setdefault(key, len(slots))
    def ref(half, dz, dx, p): return buf[half].at[at(-dz, -dx), part[p]]
    def push(half, dz, dx, axis, src=None):
        here = dz if axis == "z" else dx
        edge = 4 if axis == "z" else 2
        for sign in ((1, -1) if here == 0 else ((1,) if here > 0 else (-1,))):
            step = here + sign
            if abs(step) > edge: continue
            ndz, ndx = (step, dx) if axis == "z" else (dz, step)
            p = "all"
            if abs(step) == edge: p = "lo" if step > 0 else "hi"
            key = (half, ndz if abs(ndz) < 4 else 4, ndx if abs(ndx) < 2 else 2, axis, step)
            dst = ref(half, dz, dx, p)
            net.send(slot(*key), dst if src is None else src.at[part[p]], dst, to[axis, sign])
    for d in range(1, NZ):
        net.send(slot("small", "z", d), small_own, small.at[place(0, 0)], at(d, 0))
    push("A", 0, 0, "z", a_own)
    push("B", 0, 0, "x", b_own)
    push("B", 0, 0, "z", b_own)
    push("A", 0, 0, "x", a_own)
    small[place(0, 0)] = small_own[...]
    A[at(0, 0)] = a_own[...]
    B[at(0, 0)] = b_own[...]
    hooks("start", None)
    seen = {}
    columns = small.at[pl.ds(x * NZ, NZ)]
    def small_columns():
        for d in range(1, NZ):
            net.wait(slot("small", "z", d), small.at[place(-d, 0)])
        for d in range(1, NX):
            net.send(slot("small", "x", d), columns, columns, at(0, d))
    def small_rest():
        for d in range(1, NX):
            net.wait(slot("small", "x", d), small.at[pl.ds(xx(-d) * NZ, NZ)])
        hooks("small", None)
    before = 0
    for k, (hops, half, dz, dx, p, axis, step) in enumerate(plan()):
        if hops != before:
            if before == 1: small_columns()
            if before == 2: small_rest()
            hooks("stage", before)
            before = hops
        net.wait(slot(half, dz, dx, axis, step), ref(half, dz, dx, p))
        seen[half, dz, dx] = seen.get((half, dz, dx), 0) + 1
        whole = p == "all" or seen[half, dz, dx] == 2
        if p == "all":
            push(half, dz, dx, axis)
        if whole:
            if half == "A" and axis == "x": push(half, dz, dx, "z")
            if half == "B" and axis == "z": push(half, dz, dx, "x")
        hooks(k, (half, dz, dx, whole))
    hooks("end", None)
    for c in net.started: c.wait_send()

WIDE = 896


def dot(a, b, precision=None):
    return jnp.dot(a, b, preferred_element_type=F32, precision=precision)


def dot_nt(a, b, precision=None):
    return lax.dot_general(a, b, NT, preferred_element_type=F32, precision=precision)


def iota(shape, axis):
    return lax.broadcasted_iota(jnp.int32, shape, axis)


def normalise(values, gain):
    centred = values - jnp.mean(values, axis=-1, keepdims=True)
    spread = jnp.mean(centred * centred, axis=-1, keepdims=True)
    return (centred * lax.rsqrt(spread + EPS) * gain).astype(BF16)


def split(values):
    high = values.astype(BF16)
    return jnp.concatenate([high, (values - high.astype(F32)).astype(BF16)], axis=1)


def over_slots(values, op):
    for shift in (64, 32, 16):
        values = op(values, pltpu.roll(values, shift, 1))
    return values


def wide_row(ref, first):
    return jnp.concatenate([ref[first + i : first + i + 1, :] for i in range(D // 128)], axis=1)


def gather_kernel(
    own,
    visible,
    space,
    qkv_hbm,
    small,
    A,
    B,
    keys,
    values,
    space_keys,
    space_values,
    rsq,
    time_kv,
    columns,
    weight,
    times,
    wide_space,
    centred,
    gained,
    sends,
    receives,
    load,
):
    fetch = pltpu.make_async_copy(qkv_hbm, weight, load)
    fetch.start()
    f = lax.axis_index("frame")
    z = f // NX
    g = wide_row(own, 16)
    HI = lax.Precision.HIGHEST
    ready = []
    state = {"small": False}
    parts = {}
    jobs = []

    def project_space(n, target, base):
        cols = pl.ds(n * 256, 256)
        target[:, cols] = dot(gained[...], weight[:, pl.ds(base + n * 256, 256)]).astype(BF16)

    def project_rows(half, steps):
        buffer, first = (A, 0) if half == "A" else (B, FRAMES * HALF)
        got, held, spots = [], [], []
        for d in steps:
            at = lax.rem(z + (NZ - d), NZ)
            spot = pl.ds(at * NX, NX)
            got.append(buffer[spot].reshape(NX * HALF, D))
            lanes = columns[spot, pl.ds(0 if half == "A" else HALF, HALF), :]
            held.append(lanes.reshape(NX * HALF, 128))
            spots.append(pl.ds(pl.multiple_of(first + at * (NX * HALF), NX * HALF), NX * HALF))
        got = jnp.concatenate(got, axis=0) if len(steps) > 1 else got[0]
        held = jnp.concatenate(held, axis=0) if len(steps) > 1 else held[0]
        slot = jnp.floor((held + 0.5) * (1.0 / PATCHES))
        patch = held - slot * PATCHES
        lane = iota(held.shape, 1).astype(F32)
        pick = jnp.concatenate(
            [(patch == lane + float(n * 128)).astype(BF16) for n in range(WIDE // 128)], axis=1
        )
        tok = got.astype(F32) + dot((slot == lane).astype(BF16), times[...])
        tok = tok + dot(pick, wide_space[...])
        normed = normalise(tok, g)
        for target, base in ((keys, D), (values, 2 * D)):
            out = dot(normed, weight[:, pl.ds(base, D)]).astype(BF16)
            for i, spot in enumerate(spots):
                target[spot, :] = out[i * NX * HALF : (i + 1) * NX * HALF]

    def small_work():
        index = jnp.concatenate(
            [small[x * NZ + k, 6:7, :] for k in range(NZ) for x in range(NX)], axis=0
        )
        turned = jnp.transpose(jnp.concatenate([index] * 4, axis=0))
        for i in range(FRAMES):
            columns[i] = jnp.broadcast_to(turned[:ROWS, i : i + 1], (ROWS, 128))
        rows = []
        for i in range(D // 128):
            rows.append(
                jnp.concatenate(
                    [small[x * NZ + k, i : i + 1, :] for k in range(NZ) for x in range(NX)], axis=0
                )
            )
        time = jnp.concatenate(rows, axis=1)
        times[pl.ds(0, FRAMES), :] = time.astype(BF16)
        times[pl.ds(FRAMES, 128 - FRAMES), :] = jnp.zeros((128 - FRAMES, D), BF16)
        a = time + wide_row(own, 8)
        a = a - jnp.mean(a, axis=-1, keepdims=True)
        ag = (a * g).astype(BF16)
        time_kv[...] = dot(ag, weight[:, pl.ds(D, 2 * D)])
        b = centred[...]
        aa = dot_nt(jnp.ones((8, D), F32), a * a, HI)[0:1, :]
        bb = jnp.sum(b * b, axis=-1, keepdims=True)
        spread = jnp.maximum(dot_nt(b, a, HI) * 2.0 + (aa + bb), 0.0) * (1.0 / D)
        rsq[...] = lax.rsqrt(spread + EPS)

    def hooks(k, event):
        if k == "start":
            wide_space[pl.ds(0, PATCHES), :] = space[...]
            wide_space[pl.ds(PATCHES, WIDE - PATCHES), :] = jnp.zeros((WIDE - PATCHES, D), BF16)
            b = space[...].astype(F32)
            b = b - jnp.mean(b, axis=-1, keepdims=True)
            centred[...] = b
            gained[...] = (b * g).astype(BF16)
            fetch.wait()
            for i in (0, 1):
                project_space(i, space_keys, D)
            jobs.append(functools.partial(project_space, 2, space_keys, D))
            for i in (0, 1, 2):
                jobs.append(functools.partial(project_space, i, space_values, 2 * D))
            return
        if k == "small":
            small_work()
            state["small"] = True
            return
        if k == "stage" or k == "end":
            for job in jobs + (ready if state["small"] else []):
                job()
            jobs.clear()
            if state["small"]:
                ready.clear()
            return
        if event is None:
            return
        half, dz, dx, whole = event
        if whole:
            done = parts.setdefault((half, abs(dz)), set())
            done.add((dz, dx))
            need = {0: 3, 4: 4}.get(abs(dz), 8)
            if len(done) == need:
                steps = (dz,) if dz in (0, 4) else (abs(dz), -abs(dz))
                ready.append(functools.partial(project_rows, half, steps))

    gather(
        Net(sends, receives),
        own.at[pl.ds(0, 8)],
        visible.at[pl.ds(0, HALF)],
        visible.at[pl.ds(HALF, HALF)],
        small,
        A,
        B,
        hooks,
    )


def gather_rows(own, visible, space, qkv):
    def shape(*dims, dtype=BF16):
        return jax.ShapeDtypeStruct(dims, dtype)

    return pl.pallas_call(
        gather_kernel,
        out_shape=[
            shape(FRAMES, 8, 128, dtype=F32),
            shape(FRAMES, HALF, D),
            shape(FRAMES, HALF, D),
            shape(VIS, D),
            shape(VIS, D),
            shape(PATCHES, D),
            shape(PATCHES, D),
            shape(PATCHES, FRAMES, dtype=F32),
            shape(FRAMES, 2 * D, dtype=F32),
            shape(FRAMES, ROWS, 128, dtype=F32),
        ],
        in_specs=[VMEM] * 3 + [pl.BlockSpec(memory_space=pl.ANY)],
        out_specs=[VMEM] * 10,
        scratch_shapes=[
            pltpu.VMEM((D, 3 * D), BF16),
            pltpu.VMEM((128, D), BF16),
            pltpu.VMEM((WIDE, D), BF16),
            pltpu.VMEM((PATCHES, D), F32),
            pltpu.VMEM((PATCHES, D), BF16),
            pltpu.SemaphoreType.DMA((96,)),
            pltpu.SemaphoreType.DMA((96,)),
            pltpu.SemaphoreType.DMA,
        ],
        compiler_params=pltpu.CompilerParams(
            collective_id=0, has_side_effects=True, vmem_limit_bytes=56 << 20
        ),
        name="gather_rows",
    )(own, visible, space, qkv)


def temporal_kernel(
    slot_row,
    patch_row,
    patch_list,
    small,
    first_hbm,
    second_hbm,
    keys_hbm,
    values_hbm,
    bk,
    bv,
    rsq,
    time_kv,
    columns,
    own,
    space,
    qkv_hbm,
    out_hbm,
    after,
    pick,
    put,
    kv,
    tokens,
    query,
    scores,
    rs,
    sees,
    top,
    rowscore,
    rowtop,
    expo,
    mixed,
    row_kv,
    is_slot,
    first,
    second,
    keys,
    values,
    qkv,
    out_weight,
    loads,
):
    fetches = [
        pltpu.make_async_copy(source, target, loads.at[i])
        for i, (source, target) in enumerate(
            (
                (first_hbm, first),
                (second_hbm, second),
                (qkv_hbm.at[:, pl.ds(0, D)], qkv),
                (keys_hbm, keys),
                (values_hbm, values),
                (out_hbm, out_weight),
            )
        )
    ]
    for fetch in fetches:
        fetch.start()
    me = lax.axis_index("frame")
    m = wide_row(own, 8)
    g = wide_row(own, 16)
    step = 256
    real = pl.ds(0, PATCHES)
    for i in range(VIS // step):
        part = pl.ds(i * step, step)
        lane = iota((step, 128), 1).astype(F32)
        half, at = divmod(i * step, FRAMES * HALF)
        held = columns[pl.ds(at // HALF, step // HALF), pl.ds(half * HALF, HALF), :]
        held = held.reshape(step, 128)
        slot = jnp.floor((held + 0.5) * (1.0 / PATCHES))
        patch = held - slot * PATCHES
        for n in range(WIDE // 128):
            pick[part, pl.ds(n * 128, 128)] = (patch == lane + float(n * 128)).astype(BF16)
        is_slot[part, :] = (slot == lane).astype(BF16)
    put[...] = (patch_row[...] == iota((PATCHES, VIS), 0)).astype(BF16)
    own_head = iota((FRAMES * 16, D), 0) % 16 == iota((FRAMES * 16, D), 1) // HEAD_DIM
    for n in range(2):
        part = time_kv[:, pl.ds(n * D, D)]
        part = jnp.broadcast_to(part[:, None, :], (FRAMES, 16, D)).reshape(FRAMES * 16, D)
        kv[n] = jnp.where(own_head, part, 0.0).astype(BF16)
    r = rsq[...]
    widen = (iota((FRAMES, FRAMES * 16), 0) == iota((FRAMES, FRAMES * 16), 1) // 16).astype(BF16)
    r_hi = r.astype(BF16)
    r_lo = r - r_hi.astype(F32)
    r_mid = r_lo.astype(BF16)
    r_lo = (r_lo - r_mid.astype(F32)).astype(BF16)
    rs[...] = dot(r_hi, widen) + dot(r_mid, widen) + dot(r_lo, widen)
    seen = dot(put[...], is_slot[...])
    sees[...] = dot(seen[:, :FRAMES].astype(BF16), widen)
    own_seen = jnp.sum(jnp.where(iota((PATCHES, 128), 1) == me, seen, 0.0), axis=1, keepdims=True)
    query[pl.ds(PATCHES, WIDE - PATCHES), :] = jnp.zeros((WIDE - PATCHES, D), BF16)
    top[pl.ds(PATCHES, WIDE - PATCHES), :] = jnp.zeros((WIDE - PATCHES, 128), F32)
    mine = jnp.where(slot_row[...] == me, put[...], jnp.zeros((), BF16))
    count = FRAMES * HALF
    fetches[0].wait()
    fetches[1].wait()
    fetches[2].wait()
    placed = dot(mine[:, :count], first[...].reshape(count, D))
    placed = placed + dot(mine[:, count:], second[...].reshape(count, D))
    home = lax.rem(me, NX) * NZ + me // NX
    own_time = jnp.concatenate([small[home, i : i + 1, :] for i in range(D // 128)], axis=1)
    tokens[...] = jnp.where(own_seen > 0.5, placed, m) + own_time + space[...].astype(F32)
    own_normed = normalise(tokens[...], g)
    for n in range(3):
        cols = pl.ds(n * 256, 256)
        query[real, cols] = dot(own_normed, qkv[:, cols]).astype(BF16)
    of_head = (iota((D, 128), 0) // HEAD_DIM == iota((D, 128), 1) % 16).astype(BF16)
    to_head = (iota((128, D), 0) == iota((128, D), 1) // HEAD_DIM).astype(BF16)
    to_head2 = jnp.concatenate([to_head, to_head], axis=0)
    both = dot((query[real, :].astype(F32) * bk[...].astype(F32)).astype(BF16), of_head)
    high = jnp.full((PATCHES, 128), NEG, F32)
    for n in range(4):
        cols = pl.ds(n * 128, 128)
        scale = rs[:, cols] * SCALE
        part = dot_nt(query[real, :], kv[0, cols, :]) * scale + both * scale
        scores[:, cols] = part
        high = jnp.maximum(high, jnp.where(sees[:, cols] > 0.5, NEG, part))
    top[real, :] = over_slots(high, jnp.maximum)
    fetches[3].wait()
    top_b = top[...].astype(BF16)
    for i in range(VIS // step):
        part = pl.ds(i * step, step)
        got = dot(pick[part, :], query[...])
        rowscore[part, :] = dot((got * keys[part, :].astype(F32)).astype(BF16), of_head) * SCALE
        rowtop[part, :] = dot(pick[part, :], top_b)
    over = jnp.max(rowscore[...] - rowtop[...])
    under = jnp.min(top[real, :])

    @pl.when((over > 60.0) | (under < -1e29))
    def _():
        @pl.loop(0, VIS)
        def _(i):
            p = patch_list[i]
            top[pl.ds(p, 1), :] = jnp.maximum(top[pl.ds(p, 1), :], rowscore[pl.ds(i, 1), :])

        for i in range(VIS // step):
            part = pl.ds(i * step, step)
            rowtop[part, :] = dot(pick[part, :], top[...].astype(BF16))

    peak = top[real, :].astype(BF16).astype(F32)
    fetches[4].wait()
    fetches[5].wait()
    total = jnp.zeros((PATCHES, 128), F32)
    total_r = jnp.zeros((PATCHES, 128), F32)
    for n in range(4):
        cols = pl.ds(n * 128, 128)
        e = jnp.where(sees[:, cols] > 0.5, 0.0, jnp.exp2(scores[:, cols] - peak))
        total = total + e
        e = e * rs[:, cols]
        total_r = total_r + e
        mixed[:, cols] = e.astype(BF16)
    total = over_slots(total, jnp.add)
    total_r = over_slots(total_r, jnp.add)
    for i in range(VIS // step):
        part = pl.ds(i * step, step)
        e = jnp.exp2(rowscore[part, :] - rowtop[part, :]).astype(BF16)
        expo[part, :] = e
        row_kv[part, :] = (dot(e, to_head) * values[part, :].astype(F32)).astype(BF16)
    total = total + dot(put[...], expo[...])
    share = split(1.0 / total)
    spill = split(total_r)
    for n in range(3):
        cols = pl.ds(n * 256, 256)
        value = dot(mixed[:, pl.ds(0, 512)], kv[1, :, cols])
        value = value + dot(spill, to_head2[:, n * 256 : n * 256 + 256]) * bv[:, cols].astype(F32)
        value = value + dot(put[...], row_kv[:, cols])
        value = value * dot(share, to_head2[:, n * 256 : n * 256 + 256])
        query[real, cols] = value.astype(BF16)
    for n in range(3):
        cols = pl.ds(n * 256, 256)
        after[:, cols] = tokens[:, cols] + dot(query[real, :], out_weight[:, cols])


def temporal(slot, patch, found, own, space, qkv, out_weight):
    smem = pl.BlockSpec(memory_space=pltpu.SMEM)
    return pl.pallas_call(
        temporal_kernel,
        out_shape=jax.ShapeDtypeStruct((PATCHES, D), F32),
        in_specs=[VMEM] * 2 + [smem, VMEM] + [HBM] * 4 + [VMEM] * 7 + [HBM] * 2,
        out_specs=VMEM,
        scratch_shapes=[
            pltpu.VMEM((VIS, WIDE), BF16),
            pltpu.VMEM((PATCHES, VIS), BF16),
            pltpu.VMEM((2, FRAMES * 16, D), BF16),
            pltpu.VMEM((PATCHES, D), F32),
            pltpu.VMEM((WIDE, D), BF16),
            pltpu.VMEM((PATCHES, 512), F32),
            pltpu.VMEM((PATCHES, 512), F32),
            pltpu.VMEM((PATCHES, 512), F32),
            pltpu.VMEM((WIDE, 128), F32),
            pltpu.VMEM((VIS, 128), F32),
            pltpu.VMEM((VIS, 128), F32),
            pltpu.VMEM((VIS, 128), BF16),
            pltpu.VMEM((PATCHES, 512), BF16),
            pltpu.VMEM((VIS, D), BF16),
            pltpu.VMEM((VIS, 128), BF16),
            pltpu.VMEM((FRAMES, HALF, D), BF16),
            pltpu.VMEM((FRAMES, HALF, D), BF16),
            pltpu.VMEM((VIS, D), BF16),
            pltpu.VMEM((VIS, D), BF16),
            pltpu.VMEM((D, D), BF16),
            pltpu.VMEM((D, D), BF16),
            pltpu.SemaphoreType.DMA((6,)),
        ],
        compiler_params=pltpu.CompilerParams(vmem_limit_bytes=60 << 20),
        name="temporal",
    )(slot[None, :], patch[None, :], patch, *found, own, space, qkv, out_weight)


CHUNK = 112
UNROLL = 7


def spatial_kernel(after, params, qkv, out_weight, decoded, normed, heads, mixed):
    g = wide_row(params, 24)

    @pl.loop(0, PATCHES // CHUNK)
    def _(i):
        part = pl.ds(pl.multiple_of(i * CHUNK, CHUNK), CHUNK)
        normed[part, :] = normalise(after[part, :], g)

    heads[pl.ds(PATCHES, WIDE - PATCHES), :] = jnp.zeros((WIDE - PATCHES, 3 * D), BF16)

    @pl.loop(0, 9)
    def _(n):
        cols = pl.ds(pl.multiple_of(n * 256, 256), 256)
        scale = jnp.where(n < 3, SCALE, 1.0)
        heads[pl.ds(0, PATCHES), cols] = (dot(normed[...], qkv[:, cols]) * scale).astype(BF16)

    left = (iota((1, 128), 1) < HEAD_DIM).astype(BF16)
    right = (iota((1, 128), 1) >= HEAD_DIM).astype(BF16)
    real = (iota((WIDE, 1), 0) < PATCHES).astype(BF16)
    tail = iota((1, 128), 1) < PATCHES - (WIDE - 128)

    @pl.loop(0, HEADS // 2)
    def _(pair):
        def lanes(base):
            return pl.ds(pl.multiple_of(base + pair * 128, 128), 128)

        keys = heads[:, lanes(D)]
        values = heads[:, lanes(2 * D)]
        sides = [
            (side, jnp.concatenate([values * side, real * side], axis=1))
            for side in (left, right)
        ]

        @pl.loop(0, PATCHES // CHUNK, unroll=UNROLL)
        def _(i):
            part = pl.ds(pl.multiple_of(i * CHUNK, CHUNK), CHUNK)
            found = jnp.zeros((CHUNK, 256), F32)
            for side, value in sides:
                s = dot_nt(heads[part, lanes(0)] * side, keys)
                s = jnp.concatenate(
                    [s[:, : WIDE - 128], jnp.where(tail, s[:, WIDE - 128 :], NEG)], axis=1
                )
                s = jnp.exp2(s - jnp.max(s, axis=1, keepdims=True)).astype(BF16)
                found = found + dot(s, value)
            mixed[part, lanes(0)] = (found[:, :128] / found[:, 128:]).astype(BF16)

    @pl.loop(0, 3)
    def _(n):
        cols = pl.ds(pl.multiple_of(n * 256, 256), 256)
        decoded[:, cols] = (after[:, cols] + dot(mixed[...], out_weight[:, cols])).astype(BF16)


def spatial(after, params, qkv, out_weight):
    return pl.pallas_call(
        spatial_kernel,
        out_shape=jax.ShapeDtypeStruct((PATCHES, D), BF16),
        in_specs=[VMEM] * 4,
        out_specs=VMEM,
        scratch_shapes=[
            pltpu.VMEM((PATCHES, D), BF16),
            pltpu.VMEM((WIDE, 3 * D), BF16),
            pltpu.VMEM((PATCHES, D), BF16),
        ],
        compiler_params=pltpu.CompilerParams(vmem_limit_bytes=56 << 20),
        name="spatial",
    )(after, params, qkv, out_weight)


def body(
    visible,
    vis_index,
    mask_token,
    time_pos,
    space_pos,
    temporal_gain,
    temporal_qkv,
    temporal_out,
    spatial_gain,
    spatial_qkv,
    spatial_out,
):
    gap = jnp.zeros((256,), F32)
    own = jnp.concatenate(
        [time_pos.reshape(D).astype(F32), vis_index.astype(F32), gap[: 256 - ROWS]]
        + [mask_token.astype(F32), gap, temporal_gain.astype(F32), gap]
        + [spatial_gain.astype(F32), gap]
    ).reshape(32, 128)
    found = gather_rows(own, visible, space_pos, temporal_qkv)
    index = found[0][:, 6, :ROWS].astype(jnp.int32)
    index = index.reshape(NX, NZ, 2, HALF).transpose(2, 1, 0, 3).reshape(-1)
    slot = index // PATCHES
    patch = index - slot * PATCHES
    after = temporal(slot, patch, found, own, space_pos, temporal_qkv, temporal_out)
    return spatial(after, own, spatial_qkv, spatial_out)[None]


def solution(mesh):
    in_specs = (
        P(("clip", "frame"), None),
        P(("clip", "frame")),
        P(),
        P("frame", None),
        P(),
        P(),
        P(),
        P(),
        P(),
        P(),
        P(),
    )
    out_specs = P(("clip", "frame"), None, None)
    return jax.shard_map(body, mesh=mesh, in_specs=in_specs, out_specs=out_specs, check_vma=False)
```

```python
import functools
import math

import jax
import jax.numpy as jnp
from jax import lax
from jax.experimental import pallas as pl
from jax.experimental.pallas import tpu as pltpu
from jax.sharding import PartitionSpec as P

NX, NZ = 4, 8
FRAMES = NX * NZ
D = 768
HEADS = 12
HEAD_DIM = 64
PATCHES = 784
ROWS = 64
HALF = ROWS // 2
VIS = FRAMES * ROWS
EPS = 1e-6
SCALE = 1.0 / math.sqrt(HEAD_DIM)
NEG = -1e30
F32 = jnp.float32
BF16 = jnp.bfloat16
NT = (((1,), (1,)), ((), ()))
VMEM = pl.BlockSpec(memory_space=pltpu.VMEM)
HBM = pl.BlockSpec(memory_space=pl.ANY)


class Net:
    def __init__(self, sends, receives):
        self.sends, self.receives, self.started = sends, receives, []

    def send(self, slot, source, target, device):
        copy = pltpu.make_async_remote_copy(
            src_ref=source,
            dst_ref=target,
            send_sem=self.sends.at[slot],
            recv_sem=self.receives.at[slot],
            device_id={"frame": device},
        )
        copy.start()
        self.started.append(copy)

    def wait(self, slot, ref):
        pltpu.make_async_remote_copy(
            src_ref=ref,
            dst_ref=ref,
            send_sem=self.sends.at[slot],
            recv_sem=self.receives.at[slot],
            device_id={"frame": 0},
        ).wait_recv()


def plan():
    events = []
    for half, first in (("A", "x"), ("B", "z")):
        for dz in (0, 1, -1, 2, -2, 3, -3, 4):
            for dx in (0, 1, -1, 2):
                if dz == 0 and dx == 0: continue
                by = ("z" if dz else "x") if half == "A" else ("x" if dx else "z")
                steps = dz if by == "z" else dx
                edge = 4 if by == "z" else 2
                hops = abs(dz) + abs(dx)
                if steps == edge:
                    events.append((hops, half, dz, dx, "lo", by, edge))
                    events.append((hops, half, dz, dx, "hi", by, -edge))
                else:
                    events.append((hops, half, dz, dx, "all", by, steps))
    rank = {"A": 0, "B": 1}
    events.sort(key=lambda e: (e[0], e[5] != "z", rank[e[1]]))
    return events

def gather(net, small_own, a_own, b_own, small, A, B, hooks=lambda k, e: None):
    f = lax.axis_index("frame")
    z, x = f // NX, f % NX
    def zz(d): return lax.rem(z + (d + NZ), NZ)
    def xx(d): return lax.rem(x + (d + NX), NX)
    def place(dz, dx): return xx(dx) * NZ + zz(dz)
    def at(dz, dx): return zz(dz) * NX + xx(dx)
    to = {("x", 1): at(0, 1), ("x", -1): at(0, -1), ("z", 1): at(1, 0), ("z", -1): at(-1, 0)}
    bar = pltpu.get_barrier_semaphore()
    peers = [at(d, 0) for d in range(1, NZ)] + [at(0, d) for d in range(1, NX)]
    for n in peers:
        pl.semaphore_signal(bar, inc=1, device_id={"frame": n})
    hooks("pre", None)
    pl.semaphore_wait(bar, len(peers))
    q = HALF // 2
    part = {"lo": pl.ds(0, q), "hi": pl.ds(q, q), "all": pl.ds(0, HALF)}
    buf = {"A": A, "B": B}
    slots = {}
    def slot(*key):
        return slots.setdefault(key, len(slots))
    def ref(half, dz, dx, p): return buf[half].at[at(-dz, -dx), part[p]]
    def push(half, dz, dx, axis, src=None):
        here = dz if axis == "z" else dx
        edge = 4 if axis == "z" else 2
        for sign in ((1, -1) if here == 0 else ((1,) if here > 0 else (-1,))):
            step = here + sign
            if abs(step) > edge: continue
            ndz, ndx = (step, dx) if axis == "z" else (dz, step)
            p = "all"
            if abs(step) == edge: p = "lo" if step > 0 else "hi"
            key = (half, ndz if abs(ndz) < 4 else 4, ndx if abs(ndx) < 2 else 2, axis, step)
            dst = ref(half, dz, dx, p)
            net.send(slot(*key), dst if src is None else src.at[part[p]], dst, to[axis, sign])
    for d in range(1, NZ):
        net.send(slot("small", "z", d), small_own, small.at[place(0, 0)], at(d, 0))
    push("A", 0, 0, "z", a_own)
    push("B", 0, 0, "x", b_own)
    push("B", 0, 0, "z", b_own)
    push("A", 0, 0, "x", a_own)
    small[place(0, 0)] = small_own[...]
    A[at(0, 0)] = a_own[...]
    B[at(0, 0)] = b_own[...]
    hooks("start", None)
    seen = {}
    columns = small.at[pl.ds(x * NZ, NZ)]
    def small_columns():
        for d in range(1, NZ):
            net.wait(slot("small", "z", d), small.at[place(-d, 0)])
        for d in range(1, NX):
            net.send(slot("small", "x", d), columns, columns, at(0, d))
    def small_rest():
        for d in range(1, NX):
            net.wait(slot("small", "x", d), small.at[pl.ds(xx(-d) * NZ, NZ)])
        hooks("small", None)
    before = 0
    for k, (hops, half, dz, dx, p, axis, step) in enumerate(plan()):
        if hops != before:
            if before == 1: small_columns()
            if before == 2: small_rest()
            hooks("stage", before)
            before = hops
        net.wait(slot(half, dz, dx, axis, step), ref(half, dz, dx, p))
        seen[half, dz, dx] = seen.get((half, dz, dx), 0) + 1
        whole = p == "all" or seen[half, dz, dx] == 2
        if p == "all":
            push(half, dz, dx, axis)
        if whole:
            if half == "A" and axis == "x": push(half, dz, dx, "z")
            if half == "B" and axis == "z": push(half, dz, dx, "x")
        hooks(k, (half, dz, dx, whole))
    hooks("end", None)
    for c in net.started: c.wait_send()

WIDE = 896


def dot(a, b, precision=None):
    return jnp.dot(a, b, preferred_element_type=F32, precision=precision)


def dot_nt(a, b, precision=None):
    return lax.dot_general(a, b, NT, preferred_element_type=F32, precision=precision)


def iota(shape, axis):
    return lax.broadcasted_iota(jnp.int32, shape, axis)


def normalise(values, gain):
    centred = values - jnp.mean(values, axis=-1, keepdims=True)
    spread = jnp.mean(centred * centred, axis=-1, keepdims=True)
    return (centred * lax.rsqrt(spread + EPS) * gain).astype(BF16)


def split(values):
    high = values.astype(BF16)
    return jnp.concatenate([high, (values - high.astype(F32)).astype(BF16)], axis=1)


def over_slots(values, op):
    for shift in (64, 32, 16):
        values = op(values, pltpu.roll(values, shift, 1))
    return values


def wide_row(ref, first):
    return jnp.concatenate([ref[first + i : first + i + 1, :] for i in range(D // 128)], axis=1)


def gather_kernel(
    own,
    visible,
    space,
    qkv_hbm,
    small,
    a_hbm,
    b_hbm,
    keys_hbm,
    values_hbm,
    space_keys,
    space_values,
    rsq,
    time_kv,
    columns,
    weight,
    times,
    wide_space,
    centred,
    gained,
    A,
    B,
    keys,
    values,
    saves,
    sends,
    receives,
    load,
):
    fetch = pltpu.make_async_copy(qkv_hbm, weight, load)
    fetch.start()
    f = lax.axis_index("frame")
    z = f // NX
    g = wide_row(own, 16)
    HI = lax.Precision.HIGHEST
    ready = []
    state = {"small": False}
    parts = {}
    jobs = []
    saved = []

    def save(source, target):
        copy = pltpu.make_async_copy(source, target, saves.at[len(saved)])
        copy.start()
        saved.append(copy)


    def project_space(n, target, base):
        cols = pl.ds(n * 256, 256)
        target[:, cols] = dot(gained[...], weight[:, pl.ds(base + n * 256, 256)]).astype(BF16)

    def project_rows(half, steps):
        buffer, first = (A, 0) if half == "A" else (B, FRAMES * HALF)
        got, held, spots = [], [], []
        for d in steps:
            at = lax.rem(z + (NZ - d), NZ)
            spot = pl.ds(at * NX, NX)
            save(buffer.at[spot], (a_hbm if half == "A" else b_hbm).at[spot])
            got.append(buffer[spot].reshape(NX * HALF, D))
            lanes = columns[spot, pl.ds(0 if half == "A" else HALF, HALF), :]
            held.append(lanes.reshape(NX * HALF, 128))
            spots.append(pl.ds(pl.multiple_of(first + at * (NX * HALF), NX * HALF), NX * HALF))
        got = jnp.concatenate(got, axis=0) if len(steps) > 1 else got[0]
        held = jnp.concatenate(held, axis=0) if len(steps) > 1 else held[0]
        slot = jnp.floor((held + 0.5) * (1.0 / PATCHES))
        patch = held - slot * PATCHES
        lane = iota(held.shape, 1).astype(F32)
        pick = jnp.concatenate(
            [(patch == lane + float(n * 128)).astype(BF16) for n in range(WIDE // 128)], axis=1
        )
        tok = got.astype(F32) + dot((slot == lane).astype(BF16), times[...])
        tok = tok + dot(pick, wide_space[...])
        normed = normalise(tok, g)
        for target, base, out_hbm in ((keys, D, keys_hbm), (values, 2 * D, values_hbm)):
            out = dot(normed, weight[:, pl.ds(base, D)]).astype(BF16)
            for i, spot in enumerate(spots):
                target[spot, :] = out[i * NX * HALF : (i + 1) * NX * HALF]
                save(target.at[spot], out_hbm.at[spot])

    def small_work():
        index = jnp.concatenate(
            [small[x * NZ + k, 6:7, :] for k in range(NZ) for x in range(NX)], axis=0
        )
        turned = jnp.transpose(jnp.concatenate([index] * 4, axis=0))
        for i in range(FRAMES):
            columns[i] = jnp.broadcast_to(turned[:ROWS, i : i + 1], (ROWS, 128))
        rows = []
        for i in range(D // 128):
            rows.append(
                jnp.concatenate(
                    [small[x * NZ + k, i : i + 1, :] for k in range(NZ) for x in range(NX)], axis=0
                )
            )
        time = jnp.concatenate(rows, axis=1)
        times[pl.ds(0, FRAMES), :] = time.astype(BF16)
        times[pl.ds(FRAMES, 128 - FRAMES), :] = jnp.zeros((128 - FRAMES, D), BF16)
        a = time + wide_row(own, 8)
        a = a - jnp.mean(a, axis=-1, keepdims=True)
        ag = (a * g).astype(BF16)
        time_kv[...] = dot(ag, weight[:, pl.ds(D, 2 * D)])
        b = centred[...]
        aa = dot_nt(jnp.ones((8, D), F32), a * a, HI)[0:1, :]
        bb = jnp.sum(b * b, axis=-1, keepdims=True)
        spread = jnp.maximum(dot_nt(b, a, HI) * 2.0 + (aa + bb), 0.0) * (1.0 / D)
        rsq[...] = lax.rsqrt(spread + EPS)

    def hooks(k, event):
        if k == "start":
            wide_space[pl.ds(0, PATCHES), :] = space[...]
            wide_space[pl.ds(PATCHES, WIDE - PATCHES), :] = jnp.zeros((WIDE - PATCHES, D), BF16)
            b = space[...].astype(F32)
            b = b - jnp.mean(b, axis=-1, keepdims=True)
            centred[...] = b
            gained[...] = (b * g).astype(BF16)
            fetch.wait()
            for i in (0, 1):
                project_space(i, space_keys, D)
            jobs.append(functools.partial(project_space, 2, space_keys, D))
            for i in (0, 1, 2):
                jobs.append(functools.partial(project_space, i, space_values, 2 * D))
            return
        if k == "small":
            small_work()
            state["small"] = True
            return
        if k == "stage" or k == "end":
            for job in jobs + (ready if state["small"] else []):
                job()
            jobs.clear()
            if state["small"]:
                ready.clear()
            return
        if event is None:
            return
        half, dz, dx, whole = event
        if whole:
            done = parts.setdefault((half, abs(dz)), set())
            done.add((dz, dx))
            need = {0: 3, 4: 4}.get(abs(dz), 8)
            if len(done) == need:
                steps = (dz,) if dz in (0, 4) else (abs(dz), -abs(dz))
                ready.append(functools.partial(project_rows, half, steps))

    gather(
        Net(sends, receives),
        own.at[pl.ds(0, 8)],
        visible.at[pl.ds(0, HALF)],
        visible.at[pl.ds(HALF, HALF)],
        small,
        A,
        B,
        hooks,
    )
    for copy in saved:
        copy.wait()


def gather_rows(own, visible, space, qkv):
    def shape(*dims, dtype=BF16):
        return jax.ShapeDtypeStruct(dims, dtype)

    return pl.pallas_call(
        gather_kernel,
        out_shape=[
            shape(FRAMES, 8, 128, dtype=F32),
            shape(FRAMES, HALF, D),
            shape(FRAMES, HALF, D),
            shape(VIS, D),
            shape(VIS, D),
            shape(PATCHES, D),
            shape(PATCHES, D),
            shape(PATCHES, FRAMES, dtype=F32),
            shape(FRAMES, 2 * D, dtype=F32),
            shape(FRAMES, ROWS, 128, dtype=F32),
        ],
        in_specs=[VMEM] * 3 + [pl.BlockSpec(memory_space=pl.ANY)],
        out_specs=[VMEM] + [HBM] * 4 + [VMEM] * 5,
        scratch_shapes=[
            pltpu.VMEM((D, 3 * D), BF16),
            pltpu.VMEM((128, D), BF16),
            pltpu.VMEM((WIDE, D), BF16),
            pltpu.VMEM((PATCHES, D), F32),
            pltpu.VMEM((PATCHES, D), BF16),
            pltpu.VMEM((FRAMES, HALF, D), BF16),
            pltpu.VMEM((FRAMES, HALF, D), BF16),
            pltpu.VMEM((VIS, D), BF16),
            pltpu.VMEM((VIS, D), BF16),
            pltpu.SemaphoreType.DMA((48,)),
            pltpu.SemaphoreType.DMA((96,)),
            pltpu.SemaphoreType.DMA((96,)),
            pltpu.SemaphoreType.DMA,
        ],
        compiler_params=pltpu.CompilerParams(
            collective_id=0, has_side_effects=True, vmem_limit_bytes=56 << 20
        ),
        name="gather_rows",
    )(own, visible, space, qkv)


def temporal_kernel(
    slot_row,
    patch_row,
    patch_list,
    small,
    first_hbm,
    second_hbm,
    keys_hbm,
    values_hbm,
    bk,
    bv,
    rsq,
    time_kv,
    columns,
    own,
    space,
    qkv_hbm,
    out_hbm,
    after,
    pick,
    put,
    kv,
    tokens,
    query,
    scores,
    rs,
    sees,
    top,
    rowscore,
    rowtop,
    expo,
    mixed,
    row_kv,
    is_slot,
    first,
    second,
    keys,
    values,
    qkv,
    out_weight,
    loads,
):
    fetches = [
        pltpu.make_async_copy(source, target, loads.at[i])
        for i, (source, target) in enumerate(
            (
                (first_hbm, first),
                (second_hbm, second),
                (qkv_hbm.at[:, pl.ds(0, D)], qkv),
                (keys_hbm, keys),
                (values_hbm, values),
                (out_hbm, out_weight),
            )
        )
    ]
    for fetch in fetches:
        fetch.start()
    me = lax.axis_index("frame")
    m = wide_row(own, 8)
    g = wide_row(own, 16)
    step = 256
    real = pl.ds(0, PATCHES)
    for i in range(VIS // step):
        part = pl.ds(i * step, step)
        lane = iota((step, 128), 1).astype(F32)
        half, at = divmod(i * step, FRAMES * HALF)
        held = columns[pl.ds(at // HALF, step // HALF), pl.ds(half * HALF, HALF), :]
        held = held.reshape(step, 128)
        slot = jnp.floor((held + 0.5) * (1.0 / PATCHES))
        patch = held - slot * PATCHES
        for n in range(WIDE // 128):
            pick[part, pl.ds(n * 128, 128)] = (patch == lane + float(n * 128)).astype(BF16)
        is_slot[part, :] = (slot == lane).astype(BF16)
    put[...] = (patch_row[...] == iota((PATCHES, VIS), 0)).astype(BF16)
    own_head = iota((FRAMES * 16, D), 0) % 16 == iota((FRAMES * 16, D), 1) // HEAD_DIM
    for n in range(2):
        part = time_kv[:, pl.ds(n * D, D)]
        part = jnp.broadcast_to(part[:, None, :], (FRAMES, 16, D)).reshape(FRAMES * 16, D)
        kv[n] = jnp.where(own_head, part, 0.0).astype(BF16)
    r = rsq[...]
    widen = (iota((FRAMES, FRAMES * 16), 0) == iota((FRAMES, FRAMES * 16), 1) // 16).astype(BF16)
    r_hi = r.astype(BF16)
    r_lo = r - r_hi.astype(F32)
    r_mid = r_lo.astype(BF16)
    r_lo = (r_lo - r_mid.astype(F32)).astype(BF16)
    rs[...] = dot(r_hi, widen) + dot(r_mid, widen) + dot(r_lo, widen)
    seen = dot(put[...], is_slot[...])
    sees[...] = dot(seen[:, :FRAMES].astype(BF16), widen)
    own_seen = jnp.sum(jnp.where(iota((PATCHES, 128), 1) == me, seen, 0.0), axis=1, keepdims=True)
    query[pl.ds(PATCHES, WIDE - PATCHES), :] = jnp.zeros((WIDE - PATCHES, D), BF16)
    top[pl.ds(PATCHES, WIDE - PATCHES), :] = jnp.zeros((WIDE - PATCHES, 128), F32)
    mine = jnp.where(slot_row[...] == me, put[...], jnp.zeros((), BF16))
    count = FRAMES * HALF
    fetches[0].wait()
    fetches[1].wait()
    fetches[2].wait()
    placed = dot(mine[:, :count], first[...].reshape(count, D))
    placed = placed + dot(mine[:, count:], second[...].reshape(count, D))
    home = lax.rem(me, NX) * NZ + me // NX
    own_time = jnp.concatenate([small[home, i : i + 1, :] for i in range(D // 128)], axis=1)
    tokens[...] = jnp.where(own_seen > 0.5, placed, m) + own_time + space[...].astype(F32)
    own_normed = normalise(tokens[...], g)
    for n in range(3):
        cols = pl.ds(n * 256, 256)
        query[real, cols] = dot(own_normed, qkv[:, cols]).astype(BF16)
    of_head = (iota((D, 128), 0) // HEAD_DIM == iota((D, 128), 1) % 16).astype(BF16)
    to_head = (iota((128, D), 0) == iota((128, D), 1) // HEAD_DIM).astype(BF16)
    to_head2 = jnp.concatenate([to_head, to_head], axis=0)
    both = dot((query[real, :].astype(F32) * bk[...].astype(F32)).astype(BF16), of_head)
    high = jnp.full((PATCHES, 128), NEG, F32)
    for n in range(4):
        cols = pl.ds(n * 128, 128)
        scale = rs[:, cols] * SCALE
        part = dot_nt(query[real, :], kv[0, cols, :]) * scale + both * scale
        scores[:, cols] = part
        high = jnp.maximum(high, jnp.where(sees[:, cols] > 0.5, NEG, part))
    top[real, :] = over_slots(high, jnp.maximum)
    fetches[3].wait()
    top_b = top[...].astype(BF16)
    for i in range(VIS // step):
        part = pl.ds(i * step, step)
        got = dot(pick[part, :], query[...])
        rowscore[part, :] = dot((got * keys[part, :].astype(F32)).astype(BF16), of_head) * SCALE
        rowtop[part, :] = dot(pick[part, :], top_b)
    over = jnp.max(rowscore[...] - rowtop[...])
    under = jnp.min(top[real, :])

    @pl.when((over > 40.0) | (under < -1e29))
    def _():
        @pl.loop(0, VIS)
        def _(i):
            p = patch_list[i]
            top[pl.ds(p, 1), :] = jnp.maximum(top[pl.ds(p, 1), :], rowscore[pl.ds(i, 1), :])

        for i in range(VIS // step):
            part = pl.ds(i * step, step)
            rowtop[part, :] = dot(pick[part, :], top[...].astype(BF16))

    peak = top[real, :].astype(BF16).astype(F32)
    fetches[4].wait()
    fetches[5].wait()
    total = jnp.zeros((PATCHES, 128), F32)
    total_r = jnp.zeros((PATCHES, 128), F32)
    for n in range(4):
        cols = pl.ds(n * 128, 128)
        e = jnp.where(sees[:, cols] > 0.5, 0.0, jnp.exp(scores[:, cols] - peak))
        total = total + e
        e = e * rs[:, cols]
        total_r = total_r + e
        mixed[:, cols] = e.astype(BF16)
    total = over_slots(total, jnp.add)
    total_r = over_slots(total_r, jnp.add)
    for i in range(VIS // step):
        part = pl.ds(i * step, step)
        e = jnp.exp(rowscore[part, :] - rowtop[part, :]).astype(BF16)
        expo[part, :] = e
        row_kv[part, :] = (dot(e, to_head) * values[part, :].astype(F32)).astype(BF16)
    total = total + dot(put[...], expo[...])
    share = split(1.0 / total)
    spill = split(total_r)
    for n in range(3):
        cols = pl.ds(n * 256, 256)
        value = dot(mixed[:, pl.ds(0, 512)], kv[1, :, cols])
        value = value + dot(spill, to_head2[:, n * 256 : n * 256 + 256]) * bv[:, cols].astype(F32)
        value = value + dot(put[...], row_kv[:, cols])
        value = value * dot(share, to_head2[:, n * 256 : n * 256 + 256])
        query[real, cols] = value.astype(BF16)
    for n in range(3):
        cols = pl.ds(n * 256, 256)
        after[:, cols] = tokens[:, cols] + dot(query[real, :], out_weight[:, cols])


def temporal(slot, patch, found, own, space, qkv, out_weight):
    smem = pl.BlockSpec(memory_space=pltpu.SMEM)
    return pl.pallas_call(
        temporal_kernel,
        out_shape=jax.ShapeDtypeStruct((PATCHES, D), F32),
        in_specs=[VMEM] * 2 + [smem, VMEM] + [HBM] * 4 + [VMEM] * 7 + [HBM] * 2,
        out_specs=VMEM,
        scratch_shapes=[
            pltpu.VMEM((VIS, WIDE), BF16),
            pltpu.VMEM((PATCHES, VIS), BF16),
            pltpu.VMEM((2, FRAMES * 16, D), BF16),
            pltpu.VMEM((PATCHES, D), F32),
            pltpu.VMEM((WIDE, D), BF16),
            pltpu.VMEM((PATCHES, 512), F32),
            pltpu.VMEM((PATCHES, 512), F32),
            pltpu.VMEM((PATCHES, 512), F32),
            pltpu.VMEM((WIDE, 128), F32),
            pltpu.VMEM((VIS, 128), F32),
            pltpu.VMEM((VIS, 128), F32),
            pltpu.VMEM((VIS, 128), BF16),
            pltpu.VMEM((PATCHES, 512), BF16),
            pltpu.VMEM((VIS, D), BF16),
            pltpu.VMEM((VIS, 128), BF16),
            pltpu.VMEM((FRAMES, HALF, D), BF16),
            pltpu.VMEM((FRAMES, HALF, D), BF16),
            pltpu.VMEM((VIS, D), BF16),
            pltpu.VMEM((VIS, D), BF16),
            pltpu.VMEM((D, D), BF16),
            pltpu.VMEM((D, D), BF16),
            pltpu.SemaphoreType.DMA((6,)),
        ],
        compiler_params=pltpu.CompilerParams(vmem_limit_bytes=60 << 20),
        name="temporal",
    )(slot[None, :], patch[None, :], patch, *found, own, space, qkv, out_weight)


CHUNK = 112
UNROLL = 7


def spatial_kernel(
    after, params, qkv_hbm, out_hbm, decoded, normed, heads, mixed, qkv, out_weight, loads
):
    fetches = [
        pltpu.make_async_copy(qkv_hbm, qkv, loads.at[0]),
        pltpu.make_async_copy(out_hbm, out_weight, loads.at[1]),
    ]
    for fetch in fetches:
        fetch.start()
    g = wide_row(params, 24)

    @pl.loop(0, PATCHES // CHUNK)
    def _(i):
        part = pl.ds(pl.multiple_of(i * CHUNK, CHUNK), CHUNK)
        normed[part, :] = normalise(after[part, :], g)

    heads[pl.ds(PATCHES, WIDE - PATCHES), :] = jnp.zeros((WIDE - PATCHES, 3 * D), BF16)

    fetches[0].wait()

    @pl.loop(0, 9, unroll=3)
    def _(n):
        cols = pl.ds(pl.multiple_of(n * 256, 256), 256)
        scale = jnp.where(n < 3, SCALE, 1.0)
        heads[pl.ds(0, PATCHES), cols] = (dot(normed[...], qkv[:, cols]) * scale).astype(BF16)

    left = (iota((1, 128), 1) < HEAD_DIM).astype(BF16)
    right = (iota((1, 128), 1) >= HEAD_DIM).astype(BF16)
    real = (iota((WIDE, 1), 0) < PATCHES).astype(BF16)
    tail = iota((1, 128), 1) < PATCHES - (WIDE - 128)

    @pl.loop(0, HEADS // 2)
    def _(pair):
        def lanes(base):
            return pl.ds(pl.multiple_of(base + pair * 128, 128), 128)

        keys = heads[:, lanes(D)]
        values = heads[:, lanes(2 * D)]
        value = jnp.concatenate(
            [
                jnp.concatenate([values * left, real * left], axis=1),
                jnp.concatenate([values * right, real * right], axis=1),
            ],
            axis=0,
        )

        @pl.loop(0, PATCHES // CHUNK, unroll=UNROLL)
        def _(i):
            part = pl.ds(pl.multiple_of(i * CHUNK, CHUNK), CHUNK)
            query = heads[part, lanes(0)]
            s = dot_nt(jnp.concatenate([query * left, query * right], axis=0), keys)
            s = jnp.concatenate(
                [s[:, : WIDE - 128], jnp.where(tail, s[:, WIDE - 128 :], NEG)], axis=1
            )
            s = jnp.exp(s - jnp.max(s, axis=1, keepdims=True)).astype(BF16)
            found = dot(jnp.concatenate([s[:CHUNK], s[CHUNK:]], axis=1), value)
            mixed[part, lanes(0)] = (found[:, :128] / found[:, 128:]).astype(BF16)

    fetches[1].wait()

    @pl.loop(0, 3, unroll=3)
    def _(n):
        cols = pl.ds(pl.multiple_of(n * 256, 256), 256)
        decoded[:, cols] = (after[:, cols] + dot(mixed[...], out_weight[:, cols])).astype(BF16)


def spatial(after, params, qkv, out_weight):
    return pl.pallas_call(
        spatial_kernel,
        out_shape=jax.ShapeDtypeStruct((PATCHES, D), BF16),
        in_specs=[VMEM] * 2 + [HBM] * 2,
        out_specs=VMEM,
        scratch_shapes=[
            pltpu.VMEM((PATCHES, D), BF16),
            pltpu.VMEM((WIDE, 3 * D), BF16),
            pltpu.VMEM((PATCHES, D), BF16),
            pltpu.VMEM((D, 3 * D), BF16),
            pltpu.VMEM((D, D), BF16),
            pltpu.SemaphoreType.DMA((2,)),
        ],
        compiler_params=pltpu.CompilerParams(vmem_limit_bytes=56 << 20),
        name="spatial",
    )(after, params, qkv, out_weight)


def body(
    visible,
    vis_index,
    mask_token,
    time_pos,
    space_pos,
    temporal_gain,
    temporal_qkv,
    temporal_out,
    spatial_gain,
    spatial_qkv,
    spatial_out,
):
    gap = jnp.zeros((256,), F32)
    own = jnp.concatenate(
        [time_pos.reshape(D).astype(F32), vis_index.astype(F32), gap[: 256 - ROWS]]
        + [mask_token.astype(F32), gap, temporal_gain.astype(F32), gap]
        + [spatial_gain.astype(F32), gap]
    ).reshape(32, 128)
    found = gather_rows(own, visible, space_pos, temporal_qkv)
    index = found[0][:, 6, :ROWS].astype(jnp.int32)
    index = index.reshape(NX, NZ, 2, HALF).transpose(2, 1, 0, 3).reshape(-1)
    slot = index // PATCHES
    patch = index - slot * PATCHES
    after = temporal(slot, patch, found, own, space_pos, temporal_qkv, temporal_out)
    return spatial(after, own, spatial_qkv, spatial_out)[None]


def solution(mesh):
    in_specs = (
        P(("clip", "frame"), None),
        P(("clip", "frame")),
        P(),
        P("frame", None),
        P(),
        P(),
        P(),
        P(),
        P(),
        P(),
        P(),
    )
    out_specs = P(("clip", "frame"), None, None)
    return jax.shard_map(body, mesh=mesh, in_specs=in_specs, out_specs=out_specs, check_vma=False)
```

```python
import functools
import math

import jax
import jax.numpy as jnp
from jax import lax
from jax.experimental import pallas as pl
from jax.experimental.pallas import tpu as pltpu
from jax.sharding import PartitionSpec as P

NX, NZ = 4, 8
FRAMES = NX * NZ
D = 768
HEADS = 12
HEAD_DIM = 64
PATCHES = 784
ROWS = 64
HALF = ROWS // 2
VIS = FRAMES * ROWS
EPS = 1e-6
SCALE = 1.0 / math.sqrt(HEAD_DIM)
NEG = -1e30
F32 = jnp.float32
BF16 = jnp.bfloat16
NT = (((1,), (1,)), ((), ()))
VMEM = pl.BlockSpec(memory_space=pltpu.VMEM)
HBM = pl.BlockSpec(memory_space=pl.ANY)


class Net:
    def __init__(self, sends, receives):
        self.sends, self.receives, self.started = sends, receives, []

    def send(self, slot, source, target, device):
        copy = pltpu.make_async_remote_copy(
            src_ref=source,
            dst_ref=target,
            send_sem=self.sends.at[slot],
            recv_sem=self.receives.at[slot],
            device_id={"frame": device},
        )
        copy.start()
        self.started.append(copy)

    def wait(self, slot, ref):
        pltpu.make_async_remote_copy(
            src_ref=ref,
            dst_ref=ref,
            send_sem=self.sends.at[slot],
            recv_sem=self.receives.at[slot],
            device_id={"frame": 0},
        ).wait_recv()


def plan():
    events = []
    for half, first in (("A", "x"), ("B", "z")):
        for dz in (0, 1, -1, 2, -2, 3, -3, 4):
            for dx in (0, 1, -1, 2):
                if dz == 0 and dx == 0: continue
                by = ("z" if dz else "x") if half == "A" else ("x" if dx else "z")
                steps = dz if by == "z" else dx
                edge = 4 if by == "z" else 2
                hops = abs(dz) + abs(dx)
                if steps == edge:
                    events.append((hops, half, dz, dx, "lo", by, edge))
                    events.append((hops, half, dz, dx, "hi", by, -edge))
                else:
                    events.append((hops, half, dz, dx, "all", by, steps))
    rank = {"A": 0, "B": 1}
    events.sort(key=lambda e: (e[0], e[5] != "z", rank[e[1]]))
    return events

def gather(net, small_own, a_own, b_own, small, A, B, hooks=lambda k, e: None):
    f = lax.axis_index("frame")
    z, x = f // NX, f % NX
    def zz(d): return lax.rem(z + (d + NZ), NZ)
    def xx(d): return lax.rem(x + (d + NX), NX)
    def place(dz, dx): return xx(dx) * NZ + zz(dz)
    def at(dz, dx): return zz(dz) * NX + xx(dx)
    to = {("x", 1): at(0, 1), ("x", -1): at(0, -1), ("z", 1): at(1, 0), ("z", -1): at(-1, 0)}
    bar = pltpu.get_barrier_semaphore()
    peers = [at(d, 0) for d in range(1, NZ)] + [at(0, d) for d in range(1, NX)]
    for n in peers:
        pl.semaphore_signal(bar, inc=1, device_id={"frame": n})
    hooks("pre", None)
    pl.semaphore_wait(bar, len(peers))
    q = HALF // 2
    part = {"lo": pl.ds(0, q), "hi": pl.ds(q, q), "all": pl.ds(0, HALF)}
    buf = {"A": A, "B": B}
    slots = {}
    def slot(*key):
        return slots.setdefault(key, len(slots))
    def ref(half, dz, dx, p): return buf[half].at[at(-dz, -dx), part[p]]
    def push(half, dz, dx, axis, src=None):
        here = dz if axis == "z" else dx
        edge = 4 if axis == "z" else 2
        for sign in ((1, -1) if here == 0 else ((1,) if here > 0 else (-1,))):
            step = here + sign
            if abs(step) > edge: continue
            ndz, ndx = (step, dx) if axis == "z" else (dz, step)
            p = "all"
            if abs(step) == edge: p = "lo" if step > 0 else "hi"
            key = (half, ndz if abs(ndz) < 4 else 4, ndx if abs(ndx) < 2 else 2, axis, step)
            dst = ref(half, dz, dx, p)
            net.send(slot(*key), dst if src is None else src.at[part[p]], dst, to[axis, sign])
    for d in range(1, NZ):
        net.send(slot("small", "z", d), small_own, small.at[place(0, 0)], at(d, 0))
    push("A", 0, 0, "z", a_own)
    push("B", 0, 0, "x", b_own)
    push("B", 0, 0, "z", b_own)
    push("A", 0, 0, "x", a_own)
    small[place(0, 0)] = small_own[...]
    A[at(0, 0)] = a_own[...]
    B[at(0, 0)] = b_own[...]
    hooks("start", None)
    seen = {}
    columns = small.at[pl.ds(x * NZ, NZ)]
    def small_columns():
        for d in range(1, NZ):
            net.wait(slot("small", "z", d), small.at[place(-d, 0)])
        for d in range(1, NX):
            net.send(slot("small", "x", d), columns, columns, at(0, d))
    def small_rest():
        for d in range(1, NX):
            net.wait(slot("small", "x", d), small.at[pl.ds(xx(-d) * NZ, NZ)])
        hooks("small", None)
    before = 0
    for k, (hops, half, dz, dx, p, axis, step) in enumerate(plan()):
        if hops != before:
            if before == 1: small_columns()
            if before == 2: small_rest()
            hooks("stage", before)
            before = hops
        net.wait(slot(half, dz, dx, axis, step), ref(half, dz, dx, p))
        seen[half, dz, dx] = seen.get((half, dz, dx), 0) + 1
        whole = p == "all" or seen[half, dz, dx] == 2
        if p == "all":
            push(half, dz, dx, axis)
        if whole:
            if half == "A" and axis == "x": push(half, dz, dx, "z")
            if half == "B" and axis == "z": push(half, dz, dx, "x")
        hooks(k, (half, dz, dx, whole))
    hooks("end", None)
    for c in net.started: c.wait_send()

WIDE = 896


def dot(a, b, precision=None):
    return jnp.dot(a, b, preferred_element_type=F32, precision=precision)


def dot_nt(a, b, precision=None):
    return lax.dot_general(a, b, NT, preferred_element_type=F32, precision=precision)


def iota(shape, axis):
    return lax.broadcasted_iota(jnp.int32, shape, axis)


def normalise(values, gain):
    centred = values - jnp.mean(values, axis=-1, keepdims=True)
    spread = jnp.mean(centred * centred, axis=-1, keepdims=True)
    return (centred * lax.rsqrt(spread + EPS) * gain).astype(BF16)


def split(values):
    high = values.astype(BF16)
    return jnp.concatenate([high, (values - high.astype(F32)).astype(BF16)], axis=1)


def over_slots(values, op):
    for shift in (64, 32, 16):
        values = op(values, pltpu.roll(values, shift, 1))
    return values


def wide_row(ref, first):
    return jnp.concatenate([ref[first + i : first + i + 1, :] for i in range(D // 128)], axis=1)


def gather_kernel(
    own,
    visible,
    space,
    qkv_hbm,
    small,
    a_hbm,
    b_hbm,
    keys_hbm,
    values_hbm,
    space_keys,
    space_values,
    rsq,
    time_kv,
    columns,
    weight,
    times,
    wide_space,
    centred,
    gained,
    A,
    B,
    keys,
    values,
    saves,
    sends,
    receives,
    load,
):
    fetch = pltpu.make_async_copy(qkv_hbm, weight, load)
    fetch.start()
    f = lax.axis_index("frame")
    z = f // NX
    g = wide_row(own, 16)
    HI = lax.Precision.HIGHEST
    ready = []
    state = {"small": False}
    parts = {}
    jobs = []
    saved = []

    def save(source, target):
        copy = pltpu.make_async_copy(source, target, saves.at[len(saved)])
        copy.start()
        saved.append(copy)


    def project_space(n, target, base):
        cols = pl.ds(n * 256, 256)
        target[:, cols] = dot(gained[...], weight[:, pl.ds(base + n * 256, 256)]).astype(BF16)

    def project_rows(half, steps):
        buffer, first = (A, 0) if half == "A" else (B, FRAMES * HALF)
        got, held, spots = [], [], []
        for d in steps:
            at = lax.rem(z + (NZ - d), NZ)
            spot = pl.ds(at * NX, NX)
            save(buffer.at[spot], (a_hbm if half == "A" else b_hbm).at[spot])
            got.append(buffer[spot].reshape(NX * HALF, D))
            lanes = columns[spot, pl.ds(0 if half == "A" else HALF, HALF), :]
            held.append(lanes.reshape(NX * HALF, 128))
            spots.append(pl.ds(pl.multiple_of(first + at * (NX * HALF), NX * HALF), NX * HALF))
        got = jnp.concatenate(got, axis=0) if len(steps) > 1 else got[0]
        held = jnp.concatenate(held, axis=0) if len(steps) > 1 else held[0]
        slot = jnp.floor((held + 0.5) * (1.0 / PATCHES))
        patch = held - slot * PATCHES
        lane = iota(held.shape, 1).astype(F32)
        pick = jnp.concatenate(
            [(patch == lane + float(n * 128)).astype(BF16) for n in range(WIDE // 128)], axis=1
        )
        tok = got.astype(F32) + dot((slot == lane).astype(BF16), times[...])
        tok = tok + dot(pick, wide_space[...])
        normed = normalise(tok, g)
        for target, base, out_hbm in ((keys, D, keys_hbm), (values, 2 * D, values_hbm)):
            out = dot(normed, weight[:, pl.ds(base, D)]).astype(BF16)
            for i, spot in enumerate(spots):
                target[spot, :] = out[i * NX * HALF : (i + 1) * NX * HALF]
                save(target.at[spot], out_hbm.at[spot])

    def small_work():
        index = jnp.concatenate(
            [small[x * NZ + k, 6:7, :] for k in range(NZ) for x in range(NX)], axis=0
        )
        turned = jnp.transpose(jnp.concatenate([index] * 4, axis=0))
        for i in range(FRAMES):
            columns[i] = jnp.broadcast_to(turned[:ROWS, i : i + 1], (ROWS, 128))
        rows = []
        for i in range(D // 128):
            rows.append(
                jnp.concatenate(
                    [small[x * NZ + k, i : i + 1, :] for k in range(NZ) for x in range(NX)], axis=0
                )
            )
        time = jnp.concatenate(rows, axis=1)
        times[pl.ds(0, FRAMES), :] = time.astype(BF16)
        times[pl.ds(FRAMES, 128 - FRAMES), :] = jnp.zeros((128 - FRAMES, D), BF16)
        a = time + wide_row(own, 8)
        a = a - jnp.mean(a, axis=-1, keepdims=True)
        ag = (a * g).astype(BF16)
        time_kv[...] = dot(ag, weight[:, pl.ds(D, 2 * D)])
        b = centred[...]
        aa = dot_nt(jnp.ones((8, D), F32), a * a, HI)[0:1, :]
        bb = jnp.sum(b * b, axis=-1, keepdims=True)
        spread = jnp.maximum(dot_nt(b, a, HI) * 2.0 + (aa + bb), 0.0) * (1.0 / D)
        rsq[...] = lax.rsqrt(spread + EPS)

    def hooks(k, event):
        if k == "start":
            wide_space[pl.ds(0, PATCHES), :] = space[...]
            wide_space[pl.ds(PATCHES, WIDE - PATCHES), :] = jnp.zeros((WIDE - PATCHES, D), BF16)
            b = space[...].astype(F32)
            b = b - jnp.mean(b, axis=-1, keepdims=True)
            centred[...] = b
            gained[...] = (b * g).astype(BF16)
            fetch.wait()
            for i in (0, 1):
                project_space(i, space_keys, D)
            jobs.append(functools.partial(project_space, 2, space_keys, D))
            for i in (0, 1, 2):
                jobs.append(functools.partial(project_space, i, space_values, 2 * D))
            return
        if k == "small":
            small_work()
            state["small"] = True
            return
        if k == "stage" or k == "end":
            for job in jobs + (ready if state["small"] else []):
                job()
            jobs.clear()
            if state["small"]:
                ready.clear()
            return
        if event is None:
            return
        half, dz, dx, whole = event
        if whole:
            done = parts.setdefault((half, abs(dz)), set())
            done.add((dz, dx))
            need = {0: 3, 4: 4}.get(abs(dz), 8)
            if len(done) == need:
                steps = (dz,) if dz in (0, 4) else (abs(dz), -abs(dz))
                ready.append(functools.partial(project_rows, half, steps))

    gather(
        Net(sends, receives),
        own.at[pl.ds(0, 8)],
        visible.at[pl.ds(0, HALF)],
        visible.at[pl.ds(HALF, HALF)],
        small,
        A,
        B,
        hooks,
    )
    for copy in saved:
        copy.wait()


def gather_rows(own, visible, space, qkv):
    def shape(*dims, dtype=BF16):
        return jax.ShapeDtypeStruct(dims, dtype)

    return pl.pallas_call(
        gather_kernel,
        out_shape=[
            shape(FRAMES, 8, 128, dtype=F32),
            shape(FRAMES, HALF, D),
            shape(FRAMES, HALF, D),
            shape(VIS, D),
            shape(VIS, D),
            shape(PATCHES, D),
            shape(PATCHES, D),
            shape(PATCHES, FRAMES, dtype=F32),
            shape(FRAMES, 2 * D, dtype=F32),
            shape(FRAMES, ROWS, 128, dtype=F32),
        ],
        in_specs=[VMEM] * 3 + [pl.BlockSpec(memory_space=pl.ANY)],
        out_specs=[VMEM] + [HBM] * 4 + [VMEM] * 5,
        scratch_shapes=[
            pltpu.VMEM((D, 3 * D), BF16),
            pltpu.VMEM((128, D), BF16),
            pltpu.VMEM((WIDE, D), BF16),
            pltpu.VMEM((PATCHES, D), F32),
            pltpu.VMEM((PATCHES, D), BF16),
            pltpu.VMEM((FRAMES, HALF, D), BF16),
            pltpu.VMEM((FRAMES, HALF, D), BF16),
            pltpu.VMEM((VIS, D), BF16),
            pltpu.VMEM((VIS, D), BF16),
            pltpu.SemaphoreType.DMA((48,)),
            pltpu.SemaphoreType.DMA((96,)),
            pltpu.SemaphoreType.DMA((96,)),
            pltpu.SemaphoreType.DMA,
        ],
        compiler_params=pltpu.CompilerParams(
            collective_id=0, has_side_effects=True, vmem_limit_bytes=56 << 20
        ),
        name="gather_rows",
    )(own, visible, space, qkv)


def temporal_kernel(
    slot_row,
    patch_row,
    patch_list,
    small,
    first_hbm,
    second_hbm,
    keys_hbm,
    values_hbm,
    bk,
    bv,
    rsq,
    time_kv,
    columns,
    own,
    space,
    qkv_hbm,
    out_hbm,
    after,
    pick,
    put,
    kv,
    tokens,
    query,
    scores,
    rs,
    sees,
    top,
    rowscore,
    rowtop,
    expo,
    mixed,
    row_kv,
    is_slot,
    first,
    second,
    keys,
    values,
    qkv,
    out_weight,
    loads,
):
    fetches = [
        pltpu.make_async_copy(source, target, loads.at[i])
        for i, (source, target) in enumerate(
            (
                (first_hbm, first),
                (second_hbm, second),
                (qkv_hbm.at[:, pl.ds(0, D)], qkv),
                (keys_hbm, keys),
                (values_hbm, values),
                (out_hbm, out_weight),
            )
        )
    ]
    for fetch in fetches:
        fetch.start()
    me = lax.axis_index("frame")
    m = wide_row(own, 8)
    g = wide_row(own, 16)
    step = 256
    real = pl.ds(0, PATCHES)
    for i in range(VIS // step):
        part = pl.ds(i * step, step)
        lane = iota((step, 128), 1).astype(F32)
        half, at = divmod(i * step, FRAMES * HALF)
        held = columns[pl.ds(at // HALF, step // HALF), pl.ds(half * HALF, HALF), :]
        held = held.reshape(step, 128)
        slot = jnp.floor((held + 0.5) * (1.0 / PATCHES))
        patch = held - slot * PATCHES
        for n in range(WIDE // 128):
            pick[part, pl.ds(n * 128, 128)] = (patch == lane + float(n * 128)).astype(BF16)
        is_slot[part, :] = (slot == lane).astype(BF16)
    put[...] = (patch_row[...] == iota((PATCHES, VIS), 0)).astype(BF16)
    own_head = iota((FRAMES * 16, D), 0) % 16 == iota((FRAMES * 16, D), 1) // HEAD_DIM
    for n in range(2):
        part = time_kv[:, pl.ds(n * D, D)]
        part = jnp.broadcast_to(part[:, None, :], (FRAMES, 16, D)).reshape(FRAMES * 16, D)
        kv[n] = jnp.where(own_head, part, 0.0).astype(BF16)
    r = rsq[...]
    widen = (iota((FRAMES, FRAMES * 16), 0) == iota((FRAMES, FRAMES * 16), 1) // 16).astype(BF16)
    r_hi = r.astype(BF16)
    r_lo = r - r_hi.astype(F32)
    r_mid = r_lo.astype(BF16)
    r_lo = (r_lo - r_mid.astype(F32)).astype(BF16)
    rs[...] = dot(r_hi, widen) + dot(r_mid, widen) + dot(r_lo, widen)
    seen = dot(put[...], is_slot[...])
    sees[...] = dot(seen[:, :FRAMES].astype(BF16), widen)
    own_seen = jnp.sum(jnp.where(iota((PATCHES, 128), 1) == me, seen, 0.0), axis=1, keepdims=True)
    query[pl.ds(PATCHES, WIDE - PATCHES), :] = jnp.zeros((WIDE - PATCHES, D), BF16)
    top[pl.ds(PATCHES, WIDE - PATCHES), :] = jnp.zeros((WIDE - PATCHES, 128), F32)
    mine = jnp.where(slot_row[...] == me, put[...], jnp.zeros((), BF16))
    count = FRAMES * HALF
    fetches[0].wait()
    fetches[1].wait()
    fetches[2].wait()
    placed = dot(mine[:, :count], first[...].reshape(count, D))
    placed = placed + dot(mine[:, count:], second[...].reshape(count, D))
    home = lax.rem(me, NX) * NZ + me // NX
    own_time = jnp.concatenate([small[home, i : i + 1, :] for i in range(D // 128)], axis=1)
    tokens[...] = jnp.where(own_seen > 0.5, placed, m) + own_time + space[...].astype(F32)
    own_normed = normalise(tokens[...], g)
    for n in range(3):
        cols = pl.ds(n * 256, 256)
        query[real, cols] = dot(own_normed, qkv[:, cols]).astype(BF16)
    of_head = (iota((D, 128), 0) // HEAD_DIM == iota((D, 128), 1) % 16).astype(BF16)
    to_head = (iota((128, D), 0) == iota((128, D), 1) // HEAD_DIM).astype(BF16)
    to_head2 = jnp.concatenate([to_head, to_head], axis=0)
    both = dot((query[real, :].astype(F32) * bk[...].astype(F32)).astype(BF16), of_head)
    high = jnp.full((PATCHES, 128), NEG, F32)
    for n in range(4):
        cols = pl.ds(n * 128, 128)
        scale = rs[:, cols] * SCALE
        part = dot_nt(query[real, :], kv[0, cols, :]) * scale + both * scale
        scores[:, cols] = part
        high = jnp.maximum(high, jnp.where(sees[:, cols] > 0.5, NEG, part))
    top[real, :] = over_slots(high, jnp.maximum)
    fetches[3].wait()
    top_b = top[...].astype(BF16)
    for i in range(VIS // step):
        part = pl.ds(i * step, step)
        got = dot(pick[part, :], query[...])
        rowscore[part, :] = dot((got * keys[part, :].astype(F32)).astype(BF16), of_head) * SCALE
        rowtop[part, :] = dot(pick[part, :], top_b)
    over = jnp.max(rowscore[...] - rowtop[...])
    under = jnp.min(top[real, :])

    @pl.when((over > 40.0) | (under < -1e29))
    def _():
        @pl.loop(0, VIS)
        def _(i):
            p = patch_list[i]
            top[pl.ds(p, 1), :] = jnp.maximum(top[pl.ds(p, 1), :], rowscore[pl.ds(i, 1), :])

        for i in range(VIS // step):
            part = pl.ds(i * step, step)
            rowtop[part, :] = dot(pick[part, :], top[...].astype(BF16))

    peak = top[real, :].astype(BF16).astype(F32)
    fetches[4].wait()
    fetches[5].wait()
    total = jnp.zeros((PATCHES, 128), F32)
    total_r = jnp.zeros((PATCHES, 128), F32)
    for n in range(4):
        cols = pl.ds(n * 128, 128)
        e = jnp.where(sees[:, cols] > 0.5, 0.0, jnp.exp(scores[:, cols] - peak))
        total = total + e
        e = e * rs[:, cols]
        total_r = total_r + e
        mixed[:, cols] = e.astype(BF16)
    total = over_slots(total, jnp.add)
    total_r = over_slots(total_r, jnp.add)
    for i in range(VIS // step):
        part = pl.ds(i * step, step)
        e = jnp.exp(rowscore[part, :] - rowtop[part, :]).astype(BF16)
        expo[part, :] = e
        row_kv[part, :] = (dot(e, to_head) * values[part, :].astype(F32)).astype(BF16)
    total = total + dot(put[...], expo[...])
    share = split(1.0 / total)
    spill = split(total_r)
    for n in range(3):
        cols = pl.ds(n * 256, 256)
        value = dot(mixed[:, pl.ds(0, 512)], kv[1, :, cols])
        value = value + dot(spill, to_head2[:, n * 256 : n * 256 + 256]) * bv[:, cols].astype(F32)
        value = value + dot(put[...], row_kv[:, cols])
        value = value * dot(share, to_head2[:, n * 256 : n * 256 + 256])
        query[real, cols] = value.astype(BF16)
    for n in range(3):
        cols = pl.ds(n * 256, 256)
        after[:, cols] = tokens[:, cols] + dot(query[real, :], out_weight[:, cols])


def temporal(slot, patch, found, own, space, qkv, out_weight):
    smem = pl.BlockSpec(memory_space=pltpu.SMEM)
    return pl.pallas_call(
        temporal_kernel,
        out_shape=jax.ShapeDtypeStruct((PATCHES, D), F32),
        in_specs=[VMEM] * 2 + [smem, VMEM] + [HBM] * 4 + [VMEM] * 7 + [HBM] * 2,
        out_specs=VMEM,
        scratch_shapes=[
            pltpu.VMEM((VIS, WIDE), BF16),
            pltpu.VMEM((PATCHES, VIS), BF16),
            pltpu.VMEM((2, FRAMES * 16, D), BF16),
            pltpu.VMEM((PATCHES, D), F32),
            pltpu.VMEM((WIDE, D), BF16),
            pltpu.VMEM((PATCHES, 512), F32),
            pltpu.VMEM((PATCHES, 512), F32),
            pltpu.VMEM((PATCHES, 512), F32),
            pltpu.VMEM((WIDE, 128), F32),
            pltpu.VMEM((VIS, 128), F32),
            pltpu.VMEM((VIS, 128), F32),
            pltpu.VMEM((VIS, 128), BF16),
            pltpu.VMEM((PATCHES, 512), BF16),
            pltpu.VMEM((VIS, D), BF16),
            pltpu.VMEM((VIS, 128), BF16),
            pltpu.VMEM((FRAMES, HALF, D), BF16),
            pltpu.VMEM((FRAMES, HALF, D), BF16),
            pltpu.VMEM((VIS, D), BF16),
            pltpu.VMEM((VIS, D), BF16),
            pltpu.VMEM((D, D), BF16),
            pltpu.VMEM((D, D), BF16),
            pltpu.SemaphoreType.DMA((6,)),
        ],
        compiler_params=pltpu.CompilerParams(vmem_limit_bytes=60 << 20),
        name="temporal",
    )(slot[None, :], patch[None, :], patch, *found, own, space, qkv, out_weight)


CHUNK = 112
UNROLL = 7


def spatial_kernel(
    after, params, qkv_hbm, out_hbm, decoded, normed, heads, mixed, qkv, out_weight, loads
):
    fetches = [
        pltpu.make_async_copy(qkv_hbm, qkv, loads.at[0]),
        pltpu.make_async_copy(out_hbm, out_weight, loads.at[1]),
    ]
    for fetch in fetches:
        fetch.start()
    g = wide_row(params, 24)

    @pl.loop(0, PATCHES // CHUNK, unroll=UNROLL)
    def _(i):
        part = pl.ds(pl.multiple_of(i * CHUNK, CHUNK), CHUNK)
        normed[part, :] = normalise(after[part, :], g)

    heads[pl.ds(PATCHES, WIDE - PATCHES), :] = jnp.zeros((WIDE - PATCHES, 3 * D), BF16)

    fetches[0].wait()

    @pl.loop(0, 9, unroll=3)
    def _(n):
        cols = pl.ds(pl.multiple_of(n * 256, 256), 256)
        scale = jnp.where(n < 3, SCALE, 1.0)
        heads[pl.ds(0, PATCHES), cols] = (dot(normed[...], qkv[:, cols]) * scale).astype(BF16)

    left = (iota((1, 128), 1) < HEAD_DIM).astype(BF16)
    right = (iota((1, 128), 1) >= HEAD_DIM).astype(BF16)
    real = (iota((WIDE, 1), 0) < PATCHES).astype(BF16)
    tail = iota((1, 128), 1) < PATCHES - (WIDE - 128)

    @pl.loop(0, HEADS // 2, unroll=2)
    def _(pair):
        def lanes(base):
            return pl.ds(pl.multiple_of(base + pair * 128, 128), 128)

        keys = heads[:, lanes(D)]
        values = heads[:, lanes(2 * D)]
        value = jnp.concatenate(
            [
                jnp.concatenate([values * left, real * left], axis=1),
                jnp.concatenate([values * right, real * right], axis=1),
            ],
            axis=0,
        )

        @pl.loop(0, PATCHES // CHUNK, unroll=UNROLL)
        def _(i):
            part = pl.ds(pl.multiple_of(i * CHUNK, CHUNK), CHUNK)
            query = heads[part, lanes(0)]
            s = dot_nt(jnp.concatenate([query * left, query * right], axis=0), keys)
            s = jnp.concatenate(
                [s[:, : WIDE - 128], jnp.where(tail, s[:, WIDE - 128 :], NEG)], axis=1
            )
            s = jnp.exp(s - jnp.max(s, axis=1, keepdims=True)).astype(BF16)
            found = dot(jnp.concatenate([s[:CHUNK], s[CHUNK:]], axis=1), value)
            mixed[part, lanes(0)] = (found[:, :128] / found[:, 128:]).astype(BF16)

    fetches[1].wait()

    @pl.loop(0, 3, unroll=3)
    def _(n):
        cols = pl.ds(pl.multiple_of(n * 256, 256), 256)
        decoded[:, cols] = (after[:, cols] + dot(mixed[...], out_weight[:, cols])).astype(BF16)


def spatial(after, params, qkv, out_weight):
    return pl.pallas_call(
        spatial_kernel,
        out_shape=jax.ShapeDtypeStruct((PATCHES, D), BF16),
        in_specs=[VMEM] * 2 + [HBM] * 2,
        out_specs=VMEM,
        scratch_shapes=[
            pltpu.VMEM((PATCHES, D), BF16),
            pltpu.VMEM((WIDE, 3 * D), BF16),
            pltpu.VMEM((PATCHES, D), BF16),
            pltpu.VMEM((D, 3 * D), BF16),
            pltpu.VMEM((D, D), BF16),
            pltpu.SemaphoreType.DMA((2,)),
        ],
        compiler_params=pltpu.CompilerParams(vmem_limit_bytes=56 << 20),
        name="spatial",
    )(after, params, qkv, out_weight)


def body(
    visible,
    vis_index,
    mask_token,
    time_pos,
    space_pos,
    temporal_gain,
    temporal_qkv,
    temporal_out,
    spatial_gain,
    spatial_qkv,
    spatial_out,
):
    gap = jnp.zeros((256,), F32)
    own = jnp.concatenate(
        [time_pos.reshape(D).astype(F32), vis_index.astype(F32), gap[: 256 - ROWS]]
        + [mask_token.astype(F32), gap, temporal_gain.astype(F32), gap]
        + [spatial_gain.astype(F32), gap]
    ).reshape(32, 128)
    found = gather_rows(own, visible, space_pos, temporal_qkv)
    index = found[0][:, 6, :ROWS].astype(jnp.int32)
    index = index.reshape(NX, NZ, 2, HALF).transpose(2, 1, 0, 3).reshape(-1)
    slot = index // PATCHES
    patch = index - slot * PATCHES
    after = temporal(slot, patch, found, own, space_pos, temporal_qkv, temporal_out)
    return spatial(after, own, spatial_qkv, spatial_out)[None]


def solution(mesh):
    in_specs = (
        P(("clip", "frame"), None),
        P(("clip", "frame")),
        P(),
        P("frame", None),
        P(),
        P(),
        P(),
        P(),
        P(),
        P(),
        P(),
    )
    out_specs = P(("clip", "frame"), None, None)
    return jax.shard_map(body, mesh=mesh, in_specs=in_specs, out_specs=out_specs, check_vma=False)
```
